256 devices in a mesh: gz: 32 (over z_lo, x, core), gy: 8 (over z_hi, y).
Axes of the slice: x: 4, y: 4, z: 8 (z_hi: 2, z_lo: 4; z = z_hi * 4 + z_lo), core: 2. Of those that a mesh axis runs over, the one named last changes fastest.
Arguments:
- features: bfloat16 [32, 320, 96, 128], P(None, 'gz', 'gy'), may hold values from -6 to 6
- labels: int32 [320, 96, 128], P('gz', 'gy'), may hold values from 0 to 65535
- weight: bfloat16 [16, 32, 3, 3, 3], replicated, may hold values from -0.21875 to 0.21875
- conv_bias: float32 [16], replicated, may hold values from -3 to 3
Outputs:
- feature_grad: bfloat16 [32, 320, 96, 128], P(None, 'gz', 'gy')
- weight_grad: float32 [16, 32, 3, 3, 3], replicated
- bias_grad: float32 [16], replicated
- loss: float32 [], replicated
The draws below stay inside these ranges and needn't reach their ends.
All inputs are finite; a program needn't handle non-finite values.
Results may differ from the reference program's by a relative error of at most 0.0075.
Values may be sent and summed in bfloat16 or wider, within the bound.
No kernel may reach another device: no remote copies, remote signals or barrier semaphores. Data moves between devices by JAX's collectives and lax.ppermute only.
A program may use at most 128 MiB of HBM per device.

```python
import jax
import jax.numpy as jnp
from jax import lax

CH_IN = 32
EMB = 16
NX = 128
DEPTH = 320
ROWS = 96


def draw_labels(key, part):
    key_size, key_shift, key_salt = jax.random.split(key, 3)
    cell_size = jax.random.randint(key_size, (3,), 3, 14)
    phase_shift = jax.random.randint(key_shift, (3,), 0, 13)
    salt_value = jax.random.randint(key_salt, (), 1, 30000)
    z_cells = (jnp.arange(DEPTH, dtype=jnp.int32) + phase_shift[0]) // cell_size[0]
    y_cells = (jnp.arange(ROWS, dtype=jnp.int32) + phase_shift[1]) // cell_size[1]
    x_cells = (jnp.arange(NX, dtype=jnp.int32) + phase_shift[2]) // cell_size[2]
    hashed = z_cells[:, None, None] * 73856093 ^ y_cells[None, :, None] * 19349663 ^ x_cells[None, None, :] * 83492791 ^ salt_value
    return jnp.bitwise_and(hashed, 65535).astype(jnp.int32)


def block_scale(key, shape, cuts, least, top_value):
    factor_of = 1.0
    for dim, blocks in cuts:
        heights = jax.random.uniform(jax.random.fold_in(jax.random.fold_in(key, 6), dim), (blocks,), jnp.float32, least / len(cuts), top_value / len(cuts))
        factor_of = factor_of * jnp.repeat(jnp.exp(heights), shape[dim] // blocks).reshape((-1,) + (1,) * (len(shape) - 1 - dim))
    return factor_of


def normal_values(key, shape, width, limit, cuts=(), kind=jnp.bfloat16):
    drawn = jax.random.normal(key, shape, jnp.float32) * width
    if len(cuts) > 0:
        drawn = block_scale(key, shape, cuts, -0.22, 0.18) * drawn
    return jnp.clip(drawn, min=-limit, max=limit).astype(kind)


def setup_inputs(seed: int = 0) -> dict:
    splits = jax.random.split(jax.random.key(seed), 5)
    features = normal_values(splits[0], (CH_IN, DEPTH, ROWS, NX), 1.0, 6.0, ((1, 32), (2, 8)))
    labels = draw_labels(jax.random.fold_in(splits[4], 71), 0)
    weight = normal_values(splits[2], (EMB, CH_IN, 3, 3, 3), (CH_IN * 27) ** -0.5, 0.21875)
    conv_bias = normal_values(splits[3], (EMB,), 0.5, 3.0, (), jnp.float32)
    return dict(features=features, labels=labels, weight=weight, conv_bias=conv_bias)


OFFSETS = (1, 3, 9)
NUMBERS = ("NCDHW", "OIDHW", "NCDHW")


def conv_valid(padded, kernel):
    return lax.conv_general_dilated(padded[None], kernel, (1, 1, 1), "VALID", dimension_numbers=NUMBERS, preferred_element_type=jnp.float32)[0]


def weight_taps(grad_bf, feat_pad):
    plane_count, row_count, cell_count = grad_bf.shape[1], grad_bf.shape[2], grad_bf.shape[3]
    pieces = []
    for tap_index in range(27):
        shift_z, shift_y, shift_x = tap_index // 9, (tap_index // 3) % 3, tap_index % 3
        window = feat_pad[:, shift_z:shift_z + plane_count, shift_y:shift_y + row_count, shift_x:shift_x + cell_count]
        pieces.append(lax.dot_general(grad_bf, window, (((1, 2, 3), (1, 2, 3)), ((), ())), preferred_element_type=jnp.float32))
    return jnp.stack(pieces, axis=2).reshape(grad_bf.shape[0], feat_pad.shape[0], 3, 3, 3)


def reference(features, labels, weight, conv_bias):
    padded = jnp.pad(features, ((0, 0), (1, 1), (1, 1), (1, 1)))
    embedding = (conv_valid(padded, weight) + conv_bias[:, None, None, None]).astype(jnp.bfloat16)
    emb_float = embedding.astype(jnp.float32)
    gradient = jnp.zeros(emb_float.shape, jnp.float32)
    loss_sum = jnp.zeros((), jnp.float32)
    pair_count = 0
    voxels = features.shape[1] * features.shape[2] * features.shape[3]
    for axis_dim in (1, 2, 3):
        extent = embedding.shape[axis_dim]
        others = voxels // extent
        for offset in OFFSETS:
            if offset < extent:
                pair_count = pair_count + (extent - offset) * others
                lower_emb = lax.slice_in_dim(emb_float, 0, extent - offset, axis=axis_dim)
                upper_emb = lax.slice_in_dim(emb_float, offset, extent, axis=axis_dim)
                lower_lab = lax.slice_in_dim(labels, 0, extent - offset, axis=axis_dim - 1)
                upper_lab = lax.slice_in_dim(labels, offset, extent, axis=axis_dim - 1)
                logits = jnp.sum(lower_emb * upper_emb, axis=0) * 0.25
                target = (lower_lab == upper_lab).astype(jnp.float32)
                loss_sum = loss_sum + jnp.sum(jax.nn.softplus(logits) - target * logits)
                slopes = (jax.nn.sigmoid(logits) - target) * 0.25
                widths_low = [(0, 0), (0, 0), (0, 0), (0, 0)]
                widths_high = [(0, 0), (0, 0), (0, 0), (0, 0)]
                widths_low[axis_dim] = (0, offset)
                widths_high[axis_dim] = (offset, 0)
                gradient = gradient + jnp.pad(slopes[None] * upper_emb, widths_low) + jnp.pad(slopes[None] * lower_emb, widths_high)
    grad_bf = gradient.astype(jnp.bfloat16)
    weight_grad = weight_taps(grad_bf, padded) / voxels
    bias_grad = jnp.sum(grad_bf.astype(jnp.float32), axis=(1, 2, 3)) / voxels
    flipped = jnp.transpose(weight[:, :, ::-1, ::-1, ::-1], (1, 0, 2, 3, 4))
    grad_pad = jnp.pad(grad_bf, ((0, 0), (1, 1), (1, 1), (1, 1)))
    feature_grad = conv_valid(grad_pad, flipped).astype(jnp.bfloat16)
    loss = loss_sum / pair_count
    return (feature_grad, weight_grad, bias_grad, loss)
```

```python
import functools

import jax
import jax.numpy as jnp
from jax import lax
from jax.experimental import pallas as pl
from jax.experimental.pallas import tpu as pltpu
from jax.sharding import PartitionSpec as P

OFFSETS = (1, 3, 9)
REACH = 9
BF = jnp.bfloat16
F32 = jnp.float32
PARAMS = pltpu.CompilerParams(vmem_limit_bytes=48 * 1024 * 1024)
VM = pl.BlockSpec(memory_space=pltpu.VMEM)
SM = pl.BlockSpec(memory_space=pltpu.SMEM)


def call(body, outs, args, specs, scratch=(), flops=0):
    size = sum(a.size * a.dtype.itemsize for a in args)
    return pl.pallas_call(
        body,
        out_shape=outs,
        in_specs=specs,
        out_specs=jax.tree.map(lambda _: VM, outs),
        scratch_shapes=list(scratch),
        compiler_params=PARAMS,
        cost_estimate=pl.CostEstimate(flops=flops, bytes_accessed=size, transcendentals=0),
    )(*args)


def even_pairs(count):
    return [(i, i ^ 1) for i in range(count - count % 2)]


def odd_pairs(count):
    pairs = [(i, i + 1) for i in range(1, count - 1, 2)]
    return pairs + [(j, i) for i, j in pairs]


def lane_shift(value, step):
    lanes = value.shape[-1]
    moved = pltpu.roll(value, (-step) % lanes, value.ndim - 1)
    lane = lax.broadcasted_iota(jnp.int32, value.shape, value.ndim - 1)
    keep = (lane < lanes - step) if step > 0 else (lane >= -step)
    return jnp.where(keep, moved, 0)


def pair_terms(logits, same):
    target = same.astype(F32)
    small = jnp.exp(-jnp.abs(logits))
    inverse = 1.0 / (1.0 + small)
    sigmoid = jnp.where(logits >= 0, inverse, small * inverse)
    slopes = (sigmoid - target) * 0.25
    losses = jnp.maximum(logits, 0.0) + jnp.log(1.0 + small) - target * logits
    return slopes, losses


def dots(left, right):
    return jnp.sum(left * right, axis=1) * 0.25


def fill_rim(ext, own_ref, ze, zo, ye, yo, pz, py, planes, rows):
    ext[1 : planes + 1, 1 : rows + 1] = own_ref[...]
    ext[(1 - pz) * (planes + 1), 1 : rows + 1] = ze[...]
    ext[pz * (planes + 1), 1 : rows + 1] = zo[...]
    ext[:, (1 - py) * (rows + 1)] = ye[...]
    ext[:, py * (rows + 1)] = yo[...]


def conv_rows(ext, w_ref, z, y, width):
    stack = [
        jnp.concatenate([ext[z + a, y + i + b] for i in range(width)], axis=1)
        for a in range(3)
        for b in range(3)
    ]
    sums = jnp.dot(w_ref[...], jnp.concatenate(stack, axis=0), preferred_element_type=F32)
    third = sums.shape[0] // 3
    lanes = sums.shape[1] // width
    for i in range(width):
        part = sums[:, i * lanes : (i + 1) * lanes]
        yield (
            lane_shift(part[:third], -1)
            + part[third : 2 * third]
            + lane_shift(part[2 * third :], 1)
        )


def forward_kernel(pos, own, ze, zo, ye, yo, w, bias, emb, ext, se, so, te, to):
    planes, rows = own.shape[0], own.shape[1]
    pz, py = pos[0], pos[1]
    fill_rim(ext, own, ze, zo, ye, yo, pz, py, planes, rows)

    @pl.loop(0, planes)
    def _(z):
        for y in range(0, rows, 2):
            for i, value in enumerate(conv_rows(ext, w, z, y, 2)):
                emb[z, y + i] = (value + bias[...]).astype(BF)

    se[...] = emb[pl.ds((1 - pz) * (planes - REACH), REACH)]
    so[...] = emb[pl.ds(pz * (planes - REACH), REACH)]
    te[...] = emb[:, pl.ds((1 - py) * (rows - REACH), REACH)]
    to[...] = emb[:, pl.ds(py * (rows - REACH), REACH)]


def inner_kernel(emb, lab, grad, loss):
    planes, rows = emb.shape[0], emb.shape[1]
    lanes = emb.shape[3]
    lane = lax.broadcasted_iota(jnp.int32, (rows, lanes), 1)
    loss[...] = jnp.zeros_like(loss)

    @pl.loop(0, planes)
    def _(z):
        center = emb[z].astype(F32)
        here = lab[z]
        total = jnp.zeros(center.shape, F32)
        lost = jnp.zeros((rows, lanes), F32)
        for o in OFFSETS:
            if o < lanes:
                after = pltpu.roll(center, lanes - o, 2)
                before = pltpu.roll(center, o, 2)
                live = lane < lanes - o
                slopes, losses = pair_terms(
                    dots(center, after), here == pltpu.roll(here, lanes - o, 1)
                )
                slopes = jnp.where(live, slopes, 0.0)
                lost = lost + jnp.where(live, losses, 0.0)
                total = total + slopes[:, None, :] * after
                total = total + pltpu.roll(slopes, o, 1)[:, None, :] * before
        grad[z] = total
        for o in OFFSETS:
            if o < rows:
                low, high = center[: rows - o], center[o:]
                slopes, losses = pair_terms(dots(low, high), here[: rows - o] == here[o:])
                grad[z, : rows - o] += slopes[:, None, :] * high
                grad[z, o:] += slopes[:, None, :] * low
                loss[: rows - o] += losses
        loss[:rows] += lost

    for o in OFFSETS:

        @pl.loop(0, planes - o)
        def _(z):
            low, high = emb[z].astype(F32), emb[z + o].astype(F32)
            slopes, losses = pair_terms(dots(low, high), lab[z] == lab[z + o])
            grad[z] += slopes[:, None, :] * high
            grad[z + o] += slopes[:, None, :] * low
            loss[:rows] += losses


def outer_kernel(
    pos, emb, lab, grad, loss, ze, zo, ye, yo, labz, laby, out, shifted, fe, fo, sums
):
    planes, rows = emb.shape[0], emb.shape[1]
    pz, py = pos[0], pos[1]
    for halo, is_high in ((ze, 1 - pz), (zo, pz)):
        weight = (is_high * pos[2]).astype(F32)
        for o in OFFSETS:

            @pl.loop(0, o)
            def _(t):
                p = t + is_high * (planes - o)
                q = t + (1 - is_high) * (REACH - o)
                other = halo[q].astype(F32)
                slopes, losses = pair_terms(
                    dots(emb[p].astype(F32), other), lab[p] == labz[is_high, q]
                )
                grad[p] += slopes[:, None, :] * other
                loss[:rows] += losses * weight

    for halo, is_high in ((ye, 1 - py), (yo, py)):
        weight = (is_high * pos[3]).astype(F32)

        @pl.loop(0, planes)
        def _(z):
            for o in OFFSETS:
                p = is_high * (rows - o)
                q = (1 - is_high) * (REACH - o)
                other = halo[z, pl.ds(q, o)].astype(F32)
                mine = emb[z, pl.ds(p, o)].astype(F32)
                here = jnp.where(is_high == 1, lab[z, rows - o :], lab[z, :o])
                there = jnp.where(
                    is_high == 1, laby[1, z, :o], laby[0, z, REACH - o :]
                )
                slopes, losses = pair_terms(dots(mine, other), here == there)
                grad[z, pl.ds(p, o)] += slopes[:, None, :] * other
                loss[:o] += losses * weight

    shifted[...] = jnp.zeros_like(shifted)
    third = emb.shape[2]

    @pl.loop(0, planes)
    def _(z):
        value = grad[z].astype(BF)
        out[z] = value
        wide = value.astype(F32)
        shifted[z, 2 : rows + 2, :third] = lane_shift(wide, 1).astype(BF)
        shifted[z, 2 : rows + 2, third : 2 * third] = value
        shifted[z, 2 : rows + 2, 2 * third :] = lane_shift(wide, -1).astype(BF)

    fe[...] = out[(1 - pz) * (planes - 1)]
    fo[...] = out[pz * (planes - 1)]
    sums[...] = jnp.broadcast_to(
        jnp.sum(loss[...], keepdims=True), sums.shape
    )


def weight_kernel(shifted, ext, own, lost, out, acc):
    planes, rows = own.shape[0], own.shape[1]
    channels, lanes = own.shape[2], own.shape[3]
    acc[...] = jnp.zeros_like(acc)

    @pl.loop(0, planes)
    def _(z):
        total = acc[...]
        for y in range(0, rows + 2, 2):
            left = jnp.concatenate(
                [
                    jnp.concatenate([shifted[z, y + i + 2 - b] for b in range(3)], axis=0)
                    for i in range(2)
                ],
                axis=1,
            )
            right = jnp.concatenate(
                [
                    jnp.concatenate([ext[z + a, y + i] for a in range(3)], axis=0)
                    for i in range(2)
                ],
                axis=1,
            )
            total = total + lax.dot_general(
                left, right, (((1,), (1,)), ((), ())), preferred_element_type=F32
            )
        acc[...] = total

    height, width = acc.shape
    out[...] = jnp.zeros_like(out)
    out[:height, :width] = acc[...]
    tile = jnp.sum(own[...].astype(F32), axis=(0, 1))
    column = jnp.sum(tile, axis=1, keepdims=True)
    row = lax.broadcasted_iota(jnp.int32, (channels, lanes), 0)
    lane = lax.broadcasted_iota(jnp.int32, (channels, lanes), 1)
    line = jnp.sum(jnp.where(row == lane, column, 0.0), axis=0, keepdims=True)
    first = lax.broadcasted_iota(jnp.int32, (1, lanes), 1)
    out[height : height + 1, :] = jnp.where(first == channels, lost[0:1, :], line)


def backward_kernel(pos, own, ze, zo, ye, yo, w, out, ext):
    planes, rows = own.shape[0], own.shape[1]
    fill_rim(ext, own, ze, zo, ye, yo, pos[0], pos[1], planes, rows)

    @pl.loop(0, planes)
    def _(z):
        for y in range(0, rows, 2):
            for i, value in enumerate(conv_rows(ext, w, z, y, 2)):
                out[z, y + i] = value.astype(BF)


def final_kernel(voxels, pair_count, total, out, tail):
    groups, channels, width = out.shape
    per = groups // 3
    height = per * channels
    for a in range(3):
        part = total[:height, a * width : (a + 1) * width] * (1.0 / voxels)
        out[a * per : (a + 1) * per] = part.reshape(per, channels, width)
    line = total[height : height + 1, :]
    lane = lax.broadcasted_iota(jnp.int32, line.shape, 1)
    tail[...] = jnp.where(lane == channels, line * (1.0 / pair_count), line * (1.0 / voxels))


def rim_rows(block, low, high, index):
    own = lax.dynamic_index_in_dim(block, index, 1, keepdims=False)
    first = lax.dynamic_index_in_dim(low, index, 0)
    last = lax.dynamic_index_in_dim(high, index, 0)
    return jnp.concatenate([first, own, last], axis=0)


def swap_y(block, ze, zo, pz, py, gy):
    rows = block.shape[1]
    low = jnp.where(pz == 0, zo, ze)
    high = jnp.where(pz == 0, ze, zo)
    even = rim_rows(block, low, high, (1 - py) * (rows - 1))
    odd = rim_rows(block, low, high, py * (rows - 1))
    return (
        lax.ppermute(even, "gy", even_pairs(gy)),
        lax.ppermute(odd, "gy", odd_pairs(gy)),
    )


def total_of(value, gz, gy):
    rows = value.shape[0] // gz
    lanes = value.shape[1]
    mine = lax.all_to_all(value.reshape(gz, rows, lanes), "gz", 0, 0)
    mine = jnp.sum(mine, axis=0)
    mine = lax.all_to_all(jnp.broadcast_to(mine, (gy, rows, lanes)), "gy", 0, 0)
    mine = jnp.sum(mine, axis=0)
    mine = lax.all_to_all(jnp.broadcast_to(mine, (gz, rows, lanes)), "gz", 0, 0)
    return mine.reshape(gz * rows, lanes)


def per_device(features, labels, weight, conv_bias):
    ch_in, planes, rows, lanes = features.shape
    emb_ch = weight.shape[0]
    gz, gy = lax.axis_size("gz"), lax.axis_size("gy")
    depth, height = planes * gz, rows * gy
    voxels = depth * height * lanes
    pair_count = sum(
        (extent - o) * (voxels // extent)
        for extent in (depth, height, lanes)
        for o in OFFSETS
        if o < extent
    )
    iz, iy = lax.axis_index("gz"), lax.axis_index("gy")
    pz, py = lax.rem(iz, 2), lax.rem(iy, 2)
    pos = jnp.stack(
        [pz, py, (iz < gz - 1).astype(jnp.int32), (iy < gy - 1).astype(jnp.int32)]
    ).astype(jnp.int32)
    ze_pairs, zo_pairs = even_pairs(gz), odd_pairs(gz)
    ye_pairs, yo_pairs = even_pairs(gy), odd_pairs(gy)

    feat = jnp.transpose(features, (1, 2, 0, 3))
    taps = jnp.transpose(weight, (2, 3, 4, 0, 1))
    w_fwd = jnp.transpose(taps, (2, 3, 0, 1, 4)).reshape(3 * emb_ch, 9 * ch_in)
    w_bwd = jnp.transpose(taps[::-1, ::-1, ::-1], (2, 4, 0, 1, 3)).reshape(
        3 * ch_in, 9 * emb_ch
    )
    bias = jnp.broadcast_to(conv_bias[:, None], (emb_ch, lanes))

    fze = lax.ppermute(
        lax.dynamic_index_in_dim(feat, (1 - pz) * (planes - 1), 0, keepdims=False), "gz", ze_pairs
    )
    fzo = lax.ppermute(
        lax.dynamic_index_in_dim(feat, pz * (planes - 1), 0, keepdims=False), "gz", zo_pairs
    )
    fye, fyo = swap_y(feat, fze, fzo, pz, py, gy)

    def label_halo(dim, axis, parity, even, odd):
        room = labels.shape[dim] - REACH
        e = lax.dynamic_slice_in_dim(labels, (1 - parity) * room, REACH, dim)
        o = lax.dynamic_slice_in_dim(labels, parity * room, REACH, dim)
        e, o = lax.ppermute(e, axis, even), lax.ppermute(o, axis, odd)
        return jnp.stack([jnp.where(parity == 0, o, e), jnp.where(parity == 0, e, o)])

    labz = label_halo(0, "gz", pz, ze_pairs, zo_pairs)
    laby = label_halo(1, "gy", py, ye_pairs, yo_pairs)

    tile = (emb_ch, lanes)
    sds = jax.ShapeDtypeStruct
    conv_flops = 2 * planes * rows * lanes * 27 * ch_in * emb_ch
    emb, feat_ext, se, so, te, to = call(
        forward_kernel,
        (
            sds((planes, rows) + tile, BF),
            sds((planes + 2, rows + 2, ch_in, lanes), BF),
            sds((REACH, rows) + tile, BF),
            sds((REACH, rows) + tile, BF),
            sds((planes, REACH) + tile, BF),
            sds((planes, REACH) + tile, BF),
        ),
        (pos, feat, fze, fzo, fye, fyo, w_fwd, bias),
        [SM] + [VM] * 7,
        flops=conv_flops,
    )
    eyo = lax.ppermute(to, "gy", yo_pairs)
    eye = lax.ppermute(te, "gy", ye_pairs)
    ezo = lax.ppermute(so, "gz", zo_pairs)
    eze = lax.ppermute(se, "gz", ze_pairs)

    lost_rows = -(-rows // 8) * 8
    grad_in, loss_in = call(
        inner_kernel,
        (sds((planes, rows) + tile, F32), sds((lost_rows, lanes), F32)),
        (emb, labels),
        [VM] * 2,
        flops=conv_flops,
    )

    def outer(pos, emb, lab, g, l, ze, zo, ye, yo, lz, ly, out, shifted, fe, fo, sums, grad, loss):
        grad[...] = g[...]
        loss[...] = l[...]
        outer_kernel(
            pos, emb, lab, grad, loss, ze, zo, ye, yo, lz, ly, out, shifted, fe, fo, sums
        )

    grad, shifted, ge, go, lost = call(
        outer,
        (
            sds((planes, rows) + tile, BF),
            sds((planes, rows + 4, 3 * emb_ch, lanes), BF),
            sds((rows,) + tile, BF),
            sds((rows,) + tile, BF),
            sds((8, lanes), F32),
        ),
        (pos, emb, labels, grad_in, loss_in, eze, ezo, eye, eyo, labz, laby),
        [SM] + [VM] * 10,
        scratch=[pltpu.VMEM((planes, rows) + tile, F32), pltpu.VMEM((lost_rows, lanes), F32)],
        flops=conv_flops,
    )

    gze = lax.ppermute(ge, "gz", ze_pairs)
    gzo = lax.ppermute(go, "gz", zo_pairs)

    used = 9 * emb_ch + 1
    padded = -(-used // (8 * gz)) * 8 * gz
    partial = call(
        weight_kernel,
        sds((padded, lanes), F32),
        (shifted, feat_ext, grad, lost),
        [VM] * 4,
        scratch=[pltpu.VMEM((9 * emb_ch, 3 * ch_in), F32)],
        flops=conv_flops,
    )
    total = total_of(partial, gz, gy)

    gye, gyo = swap_y(grad, gze, gzo, pz, py, gy)
    feature_grad = call(
        backward_kernel,
        sds((planes, rows, ch_in, lanes), BF),
        (pos, grad, gze, gzo, gye, gyo, w_bwd),
        [SM] + [VM] * 6,
        scratch=[pltpu.VMEM((planes + 2, rows + 2) + tile, BF)],
        flops=conv_flops,
    )

    weight_grad, tail = call(
        functools.partial(final_kernel, voxels, pair_count),
        (sds((27, emb_ch, ch_in), F32), sds((1, lanes), F32)),
        (total,),
        [VM],
    )
    weight_grad = jnp.transpose(
        weight_grad.reshape(3, 3, 3, emb_ch, ch_in), (3, 4, 0, 1, 2)
    )
    return (
        jnp.transpose(feature_grad, (2, 0, 1, 3)),
        weight_grad,
        tail[0, :emb_ch],
        tail[0, emb_ch],
    )


def solution(mesh):
    return jax.shard_map(
        per_device,
        mesh=mesh,
        in_specs=(P(None, "gz", "gy", None), P("gz", "gy", None), P(), P()),
        out_specs=(P(None, "gz", "gy", None), P(), P(), P()),
        check_vma=False,
    )
```

```python
import functools

import jax
import jax.numpy as jnp
from jax import lax
from jax.experimental import pallas as pl
from jax.experimental.pallas import tpu as pltpu
from jax.sharding import PartitionSpec as P

OFFSETS = (1, 3, 9)
REACH = 9
BF = jnp.bfloat16
F32 = jnp.float32
PEAK = 1.15e9
PARAMS = pltpu.CompilerParams(vmem_limit_bytes=48 * 1024 * 1024)
VM = pl.BlockSpec(memory_space=pltpu.VMEM)
HELD = pl.BlockSpec(memory_space=pl.ANY)
SM = pl.BlockSpec(memory_space=pltpu.SMEM)


def call(body, outs, args, specs, scratch=(), micros=1.0, aliases={}):
    return pl.pallas_call(
        body,
        out_shape=outs,
        in_specs=specs,
        out_specs=jax.tree.map(lambda _: VM, outs),
        scratch_shapes=list(scratch),
        input_output_aliases=aliases,
        compiler_params=PARAMS,
        cost_estimate=pl.CostEstimate(
            flops=int(micros * PEAK), bytes_accessed=1, transcendentals=0
        ),
    )(*args)


def even_pairs(count):
    return [(i, i ^ 1) for i in range(count - count % 2)]


def odd_pairs(count):
    pairs = [(i, i + 1) for i in range(1, count - 1, 2)]
    return pairs + [(j, i) for i, j in pairs]


def lane_shift(value, step):
    lanes = value.shape[-1]
    moved = pltpu.roll(value, (-step) % lanes, value.ndim - 1)
    lane = lax.broadcasted_iota(jnp.int32, value.shape, value.ndim - 1)
    keep = (lane < lanes - step) if step > 0 else (lane >= -step)
    return jnp.where(keep, moved, 0)


def pair_terms(logits, same):
    target = same.astype(F32)
    small = jnp.exp(-jnp.abs(logits))
    inverse = 1.0 / (1.0 + small)
    sigmoid = jnp.where(logits >= 0, inverse, small * inverse)
    slopes = (sigmoid - target) * 0.25
    losses = jnp.maximum(logits, 0.0) + jnp.log(1.0 + small) - target * logits
    return slopes, losses


def dots(left, right):
    return jnp.sum(left * right, axis=1) * 0.25


def fill_rim(ext, ye, yo, ze, zo, pz, py, planes, rows):
    ext[1 : planes + 1, (1 - py) * (rows + 1)] = ye[...]
    ext[1 : planes + 1, py * (rows + 1)] = yo[...]
    ext[(1 - pz) * (planes + 1)] = ze[: rows + 2]
    ext[pz * (planes + 1)] = zo[: rows + 2]


def conv_rows(ext, w_ref, z, rows):
    stack = [
        jnp.concatenate([ext[z + a, y + b] for y in rows], axis=1)
        for a in range(3)
        for b in range(3)
    ]
    sums = jnp.dot(w_ref[...], jnp.concatenate(stack, axis=0), preferred_element_type=F32)
    third = sums.shape[0] // 3
    lanes = sums.shape[1] // len(rows)
    for i, y in enumerate(rows):
        part = sums[:, i * lanes : (i + 1) * lanes]
        yield (
            y,
            lane_shift(part[:third], -1)
            + part[third : 2 * third]
            + lane_shift(part[2 * third :], 1),
        )


def pack_labels(wide, blocks):
    at = 0
    for block in blocks:
        count = block.shape[0]
        wide[at : at + count] = lax.shift_right_logical(block, 8).astype(F32)
        wide[at + count : at + 2 * count] = jnp.bitwise_and(block, 255).astype(F32)
        at += 2 * count
    if at < wide.shape[0]:
        wide[at:] = jnp.zeros((wide.shape[0] - at, wide.shape[1]), F32)


def first_kernel(pos, feat, even, odd, sems):
    py, rows = pos[1], feat.shape[1]
    copies = [
        pltpu.make_async_copy(feat.at[:, (1 - py) * (rows - 1)], even, sems.at[0]),
        pltpu.make_async_copy(feat.at[:, py * (rows - 1)], odd, sems.at[1]),
    ]
    for copy in copies:
        copy.start()
    for copy in copies:
        copy.wait()


def second_kernel(pos, feat, lab, w, bias, emb, ext, even, odd, wide):
    planes, rows = feat.shape[0], feat.shape[1]
    py = pos[1]
    cells = (planes - 2) * (REACH - 1)
    ext[1 : planes + 1, 1 : rows + 1] = feat[...]
    for out, high in ((even, 1 - py), (odd, py)):
        pack_labels(
            wide,
            [
                jnp.where(high == 1, lab[z, rows - REACH :], lab[z, :REACH])
                for z in range(planes)
            ],
        )
        out[cells:] = wide[...].astype(BF).reshape(out.shape[0] - cells, *out.shape[1:])

    @pl.loop(0, planes - 2)
    def _(z):
        for y in range(0, rows - 2, 2):
            for i, value in conv_rows(feat, w, z, (y, y + 1)):
                emb[z + 1, i + 1] = (value + bias[...]).astype(BF)

    for out, high in ((even, 1 - py), (odd, py)):
        part = emb[1 : planes - 1, pl.ds(1 + high * (rows - 1 - REACH), REACH - 1)]
        out[:cells] = part.reshape(cells, *part.shape[2:])


def edge_planes(pos, own, ye, yo, even, odd):
    planes, rows = own.shape[0], own.shape[1]
    pz, py = pos[0], pos[1]
    for out, high in ((even, 1 - pz), (odd, pz)):
        plane = high * (planes - 1)
        out[1 : rows + 1] = own[plane]
        out[(1 - py) * (rows + 1)] = ye[plane]
        out[py * (rows + 1)] = yo[plane]


def third_kernel(pos, feat, ye, yo, lab, after, even, odd, wide):
    planes, rows = feat.shape[0], feat.shape[1]
    pz = pos[0]
    edge_planes(pos, feat, ye, yo, even, odd)
    for out, high in ((even, 1 - pz), (odd, pz)):
        base = high * (planes - REACH)
        pack_labels(wide, [lab[base + p] for p in range(REACH)])
        labels = wide[...].astype(BF)
        out[rows + 2 :] = labels.reshape(out.shape[0] - rows - 2, *out.shape[1:])


def forward_kernel(
    pos, part, ext_in, ye, yo, ze, zo, w, bias, emb, ext, se, so, te, to
):
    planes, rows = emb.shape[0], emb.shape[1]
    pz, py = pos[0], pos[1]
    fill_rim(ext, ye, yo, ze, zo, pz, py, planes, rows)

    @pl.loop(0, planes)
    def _(z):
        for i, value in conv_rows(ext, w, z, (0, rows - 1)):
            emb[z, i] = (value + bias[...]).astype(BF)

    @pl.loop(0, 2)
    def _(side):
        z = side * (planes - 1)
        for y in range(1, rows - 1, 2):
            for i, value in conv_rows(ext, w, z, (y, y + 1)):
                emb[z, i] = (value + bias[...]).astype(BF)

    for out, high in ((se, 1 - pz), (so, pz)):
        out[...] = emb[pl.ds(high * (planes - REACH), REACH)]
    for out, high in ((te, 1 - py), (to, py)):
        part = pl.ds(high * (rows - REACH), REACH)
        out[:REACH] = emb[0, part]
        out[REACH : 2 * REACH] = emb[planes - 1, part]
        out[2 * REACH :] = emb[1 : planes - 1, high * (rows - 1)]


def inner_kernel(pos, emb, lab, ze, zo, grad, loss, labz, widez):
    planes, rows = emb.shape[0], emb.shape[1]
    lanes = emb.shape[3]
    pz = pos[0]
    for halo, side in ((ze, 1 - pz), (zo, pz)):
        widez[...] = halo[rows + 2 :].reshape(widez.shape).astype(F32)
        for p in range(REACH):
            at = 2 * rows * p
            labz[side, p] = widez[at : at + rows] * 256.0 + widez[at + rows : at + 2 * rows]

    lane = lax.broadcasted_iota(jnp.int32, (rows, lanes), 1)
    loss[...] = jnp.zeros_like(loss)

    @pl.loop(0, planes)
    def _(z):
        center = emb[z].astype(F32)
        here = lab[z]
        total = jnp.zeros(center.shape, F32)
        lost = jnp.zeros((rows, lanes), F32)
        for o in OFFSETS:
            if o < lanes:
                after = pltpu.roll(center, lanes - o, 2)
                before = pltpu.roll(center, o, 2)
                live = lane < lanes - o
                slopes, losses = pair_terms(
                    dots(center, after), here == pltpu.roll(here, lanes - o, 1)
                )
                slopes = jnp.where(live, slopes, 0.0)
                lost = lost + jnp.where(live, losses, 0.0)
                total = total + slopes[:, None, :] * after
                total = total + pltpu.roll(slopes, o, 1)[:, None, :] * before
        grad[z] = total
        for o in OFFSETS:
            if o < rows:
                low, high = center[: rows - o], center[o:]
                slopes, losses = pair_terms(dots(low, high), here[: rows - o] == here[o:])
                grad[z, : rows - o] += slopes[:, None, :] * high
                grad[z, o:] += slopes[:, None, :] * low
                loss[: rows - o] += losses
        loss[:rows] += lost

    for o in OFFSETS:

        @pl.loop(0, planes - o)
        def _(z):
            low, high = emb[z].astype(F32), emb[z + o].astype(F32)
            slopes, losses = pair_terms(dots(low, high), lab[z] == lab[z + o])
            grad[z] += slopes[:, None, :] * high
            grad[z + o] += slopes[:, None, :] * low
            loss[:rows] += losses


def outer_kernel(
    pos,
    emb,
    lab,
    grad_in,
    loss_in,
    ze,
    zo,
    labz,
    fe,
    fo,
    ye,
    yo,
    out,
    shifted,
    ge,
    go,
    sums,
    grad,
    total,
    laby,
    wide,
    halos,
):
    planes, rows = emb.shape[0], emb.shape[1]
    pz, py = pos[0], pos[1]
    third = emb.shape[2]
    cells = (planes - 2) * (REACH - 1)
    grad[...] = grad_in[...]
    total[...] = loss_in[...]
    for halo, side in ((fe, 1 - py), (fo, py)):
        wide[...] = halo[cells:].reshape(wide.shape).astype(F32)
        for z in range(planes):
            at = 2 * REACH * z
            laby[side, z] = wide[at : at + REACH] * 256.0 + wide[at + REACH : at + 2 * REACH]

    for halo, is_high in ((ze, 1 - pz), (zo, pz)):
        weight = (is_high * pos[2]).astype(F32)
        for o in OFFSETS:

            @pl.loop(0, o)
            def _(t):
                p = t + is_high * (planes - o)
                q = t + (1 - is_high) * (REACH - o)
                other = halo[q].astype(F32)
                slopes, losses = pair_terms(
                    dots(emb[p].astype(F32), other),
                    lab[p].astype(F32) == labz[is_high, q],
                )
                grad[p] += slopes[:, None, :] * other
                total[:rows] += losses * weight

    shifted[:, :2] = jnp.zeros((planes, 2) + shifted.shape[2:], BF)
    shifted[:, rows + 2 :] = jnp.zeros((planes, 2) + shifted.shape[2:], BF)
    for early, late, is_high in ((fe, ye, 1 - py), (fo, yo, py)):
        halos[is_high, 0] = late[:REACH]
        halos[is_high, planes - 1] = late[REACH : 2 * REACH]
        halos[is_high, 1 : planes - 1, (1 - is_high) * (REACH - 1)] = late[2 * REACH :]
        part = early[: (planes - 2) * (REACH - 1)]
        halos[is_high, 1 : planes - 1, pl.ds(is_high, REACH - 1)] = part.reshape(
            planes - 2, REACH - 1, *part.shape[1:]
        )
    live = pos[3].astype(F32)

    @pl.loop(0, planes)
    def _(z):
        center = emb[z].astype(F32)
        here = lab[z].astype(F32)
        sum_z = grad[z]
        low = halos[0, z].astype(F32)
        high = halos[1, z].astype(F32)
        lower, upper = [], []
        for o in OFFSETS:
            lower.append((center[:o], low[REACH - o :], here[:o], laby[0, z, REACH - o :]))
            upper.append((center[rows - o :], high[:o], here[rows - o :], laby[1, z, :o]))
        logits = [dots(a, b) for a, b, _, _ in lower + upper]
        mine = jnp.concatenate([c for _, _, c, _ in lower + upper], axis=0)
        theirs = jnp.concatenate([d for _, _, _, d in lower + upper], axis=0)
        slopes, losses = pair_terms(jnp.concatenate(logits, axis=0), mine == theirs)
        half = sum(OFFSETS)
        total[:1] += jnp.sum(losses[half:], axis=0, keepdims=True) * live
        at = 0
        for o, (_, other, _, _) in zip(OFFSETS, lower):
            sum_z = jnp.concatenate(
                [sum_z[:o] + slopes[at : at + o, None, :] * other, sum_z[o:]], axis=0
            )
            at += o
        for o, (_, other, _, _) in zip(OFFSETS, upper):
            sum_z = jnp.concatenate(
                [
                    sum_z[: rows - o],
                    sum_z[rows - o :] + slopes[at : at + o, None, :] * other,
                ],
                axis=0,
            )
            at += o
        value = sum_z.astype(BF)
        out[z] = value
        wide = value.astype(F32)
        shifted[z, 2 : rows + 2, :third] = lane_shift(wide, 1).astype(BF)
        shifted[z, 2 : rows + 2, third : 2 * third] = value
        shifted[z, 2 : rows + 2, 2 * third :] = lane_shift(wide, -1).astype(BF)

    ge[...] = out[:, (1 - py) * (rows - 1)]
    go[...] = out[:, py * (rows - 1)]
    sums[...] = jnp.broadcast_to(jnp.sum(total[...], keepdims=True), sums.shape)


def weight_kernel(shifted, ext, own, lost, out, acc):
    planes, rows = own.shape[0], own.shape[1]
    channels, lanes = own.shape[2], own.shape[3]
    acc[...] = jnp.zeros_like(acc)

    @pl.loop(0, planes)
    def _(z):
        total = acc[...]
        for y in range(0, rows + 2, 2):
            left = jnp.concatenate(
                [
                    jnp.concatenate([shifted[z, y + i + 2 - b] for b in range(3)], axis=0)
                    for i in range(2)
                ],
                axis=1,
            )
            right = jnp.concatenate(
                [
                    jnp.concatenate([ext[z + a, y + i] for a in range(3)], axis=0)
                    for i in range(2)
                ],
                axis=1,
            )
            total = total + lax.dot_general(
                left, right, (((1,), (1,)), ((), ())), preferred_element_type=F32
            )
        acc[...] = total

    height, width = acc.shape
    out[...] = jnp.zeros_like(out)
    out[:height, :width] = acc[...]
    tile = jnp.sum(own[...].astype(F32), axis=(0, 1))
    column = jnp.sum(tile, axis=1, keepdims=True)
    row = lax.broadcasted_iota(jnp.int32, (channels, lanes), 0)
    lane = lax.broadcasted_iota(jnp.int32, (channels, lanes), 1)
    line = jnp.sum(jnp.where(row == lane, column, 0.0), axis=0, keepdims=True)
    first = lax.broadcasted_iota(jnp.int32, (1, lanes), 1)
    out[height : height + 1, :] = jnp.where(first == channels, lost[0:1, :], line)


def backward_kernel(pos, own, ye, yo, ze, zo, w, after, out, ext):
    planes, rows = own.shape[0], own.shape[1]
    ext[1 : planes + 1, 1 : rows + 1] = own[...]
    fill_rim(ext, ye, yo, ze, zo, pos[0], pos[1], planes, rows)

    @pl.loop(0, planes)
    def _(z):
        for y in range(0, rows, 2):
            for i, value in conv_rows(ext, w, z, (y, y + 1)):
                out[z, i] = value.astype(BF)


def spread_kernel(parts, out):
    out[...] = jnp.broadcast_to(jnp.sum(parts[...], axis=0), out.shape)


def final_kernel(voxels, pair_count, total, out, bias, loss):
    groups, channels, width = out.shape
    per = groups // 3
    height = per * channels
    for a in range(3):
        part = total[:height, a * width : (a + 1) * width] * (1.0 / voxels)
        out[a * per : (a + 1) * per] = part.reshape(per, channels, width)
    bias[...] = total[height : height + 1, :channels] * (1.0 / voxels)
    loss[...] = total[height : height + 1, channels : channels + 1] * (1.0 / pair_count)


def per_device(features, labels, weight, conv_bias):
    ch_in, planes, rows, lanes = features.shape
    emb_ch = weight.shape[0]
    gz, gy = lax.axis_size("gz"), lax.axis_size("gy")
    depth, height = planes * gz, rows * gy
    voxels = depth * height * lanes
    pair_count = sum(
        (extent - o) * (voxels // extent)
        for extent in (depth, height, lanes)
        for o in OFFSETS
        if o < extent
    )
    iz, iy = lax.axis_index("gz"), lax.axis_index("gy")
    pos = jnp.stack(
        [
            lax.rem(iz, 2),
            lax.rem(iy, 2),
            (iz < gz - 1).astype(jnp.int32),
            (iy < gy - 1).astype(jnp.int32),
        ]
    ).astype(jnp.int32)
    z_even, z_odd = even_pairs(gz), odd_pairs(gz)
    y_even, y_odd = even_pairs(gy), odd_pairs(gy)

    feat = jnp.transpose(features, (1, 2, 0, 3))
    taps = jnp.transpose(weight, (2, 3, 4, 0, 1))
    w_fwd = jnp.transpose(taps, (2, 3, 0, 1, 4)).reshape(3 * emb_ch, 9 * ch_in)
    w_bwd = jnp.transpose(taps[::-1, ::-1, ::-1], (2, 4, 0, 1, 3)).reshape(
        3 * ch_in, 9 * emb_ch
    )
    bias = jnp.broadcast_to(conv_bias[:, None], (emb_ch, lanes))

    sds = jax.ShapeDtypeStruct
    tile = (emb_ch, lanes)
    cells = (ch_in, lanes)
    z_blocks = -(-2 * REACH * rows // ch_in)
    y_blocks = -(-2 * REACH * planes // ch_in)

    y_message = sds((planes,) + cells, BF)
    me, mo = call(
        first_kernel, (y_message, y_message), (pos, feat), [SM, HELD],
        scratch=[pltpu.SemaphoreType.DMA((2,))],
    )
    fye = lax.ppermute(me, "gy", y_even)
    fyo = lax.ppermute(mo, "gy", y_odd)
    emb_shape = sds((planes, rows) + tile, BF)
    ext_shape = sds((planes + 2, rows + 2) + cells, BF)
    y_early = sds(
        ((planes - 2) * (REACH - 1) + y_blocks * (ch_in // emb_ch),) + tile, BF
    )
    emb_part, ext_part, me, mo = call(
        second_kernel,
        (emb_shape, ext_shape, y_early, y_early),
        (pos, feat, labels, w_fwd, bias),
        [SM] + [VM] * 4,
        scratch=[pltpu.VMEM((y_blocks * ch_in, lanes), F32)],
        micros=3.4,
    )
    aye = lax.ppermute(me, "gy", y_even)
    ayo = lax.ppermute(mo, "gy", y_odd)
    z_message = sds((rows + 2 + z_blocks,) + cells, BF)
    me, mo = call(
        third_kernel,
        (z_message, z_message),
        (pos, feat, fye, fyo, labels, me),
        [SM] + [VM] * 4 + [HELD],
        scratch=[pltpu.VMEM((z_blocks * ch_in, lanes), F32)],
    )
    fze = lax.ppermute(me, "gz", z_even)
    fzo = lax.ppermute(mo, "gz", z_odd)

    z_halo = sds((REACH, rows) + tile, BF)
    y_late = sds((2 * REACH + planes - 2,) + tile, BF)
    emb, feat_ext, se, so, te, to = call(
        forward_kernel,
        (emb_shape, ext_shape, z_halo, z_halo, y_late, y_late),
        (pos, emb_part, ext_part, fye, fyo, fze, fzo, w_fwd, bias),
        [SM] + [VM] * 8,
        micros=3.6,
        aliases={1: 0, 2: 1},
    )
    eze = lax.ppermute(se, "gz", z_even)
    ezo = lax.ppermute(so, "gz", z_odd)
    eye = lax.ppermute(te, "gy", y_even)
    eyo = lax.ppermute(to, "gy", y_odd)

    lost_rows = -(-rows // 8) * 8
    grad_shape = sds((planes, rows) + tile, F32)
    loss_shape = sds((lost_rows, lanes), F32)
    grad_a, loss_a, labz = call(
        inner_kernel,
        (
            grad_shape,
            loss_shape,
            sds((2, REACH, rows, lanes), F32),
        ),
        (pos, emb, labels, fze, fzo),
        [SM] + [VM] * 4,
        scratch=[pltpu.VMEM((z_blocks * ch_in, lanes), F32)],
        micros=6.4,
    )
    grad, shifted, ge, go, lost = call(
        outer_kernel,
        (
            sds((planes, rows) + tile, BF),
            sds((planes, rows + 4, 3 * emb_ch, lanes), BF),
            sds((planes,) + tile, BF),
            sds((planes,) + tile, BF),
            sds((8, lanes), F32),
        ),
        (pos, emb, labels, grad_a, loss_a, eze, ezo, labz, aye, ayo, eye, eyo),
        [SM] + [VM] * 11,
        scratch=[
            pltpu.VMEM((planes, rows) + tile, F32),
            pltpu.VMEM((lost_rows, lanes), F32),
            pltpu.VMEM((2, planes, REACH, lanes), F32),
            pltpu.VMEM((y_blocks * ch_in, lanes), F32),
            pltpu.VMEM((2, planes, REACH) + tile, BF),
        ],
        micros=5.0,
    )
    gye = lax.ppermute(ge, "gy", y_even)
    gyo = lax.ppermute(go, "gy", y_odd)

    used = 9 * emb_ch + 1
    padded = -(-used // (8 * gz)) * 8 * gz
    share = padded // gz
    partial = call(
        weight_kernel,
        sds((padded, lanes), F32),
        (shifted, feat_ext, grad, lost),
        [VM] * 4,
        scratch=[pltpu.VMEM((9 * emb_ch, 3 * ch_in), F32)],
        micros=3.8,
    )
    z_edge = sds((rows + 2,) + tile, BF)
    me, mo = call(edge_planes, (z_edge, z_edge), (pos, grad, gye, gyo), [SM] + [VM] * 3)
    gze = lax.ppermute(me, "gz", z_even)
    gzo = lax.ppermute(mo, "gz", z_odd)

    parts = lax.all_to_all(partial.reshape(gz, share, lanes), "gz", 0, 0)
    mine = call(spread_kernel, sds((gy, share, lanes), F32), (parts,), [VM])
    feature_grad = call(
        backward_kernel,
        sds((planes, rows) + cells, BF),
        (pos, grad, gye, gyo, gze, gzo, w_bwd, mine),
        [SM] + [VM] * 6 + [HELD],
        scratch=[pltpu.VMEM((planes + 2, rows + 2) + tile, BF)],
        micros=4.9,
    )
    parts = lax.all_to_all(mine, "gy", 0, 0)
    mine = call(spread_kernel, sds((gz, share, lanes), F32), (parts,), [VM])
    total = lax.all_to_all(mine, "gz", 0, 0).reshape(padded, lanes)

    weight_grad, bias_grad, loss = call(
        functools.partial(final_kernel, voxels, pair_count),
        (sds((27, emb_ch, ch_in), F32), sds((1, emb_ch), F32), sds((1, 1), F32)),
        (total,),
        [VM],
    )
    weight_grad = jnp.transpose(
        weight_grad.reshape(3, 3, 3, emb_ch, ch_in), (3, 4, 0, 1, 2)
    )
    return (
        jnp.transpose(feature_grad, (2, 0, 1, 3)),
        weight_grad,
        bias_grad.reshape(emb_ch),
        loss.reshape(()),
    )


def solution(mesh):
    return jax.shard_map(
        per_device,
        mesh=mesh,
        in_specs=(P(None, "gz", "gy", None), P("gz", "gy", None), P(), P()),
        out_specs=(P(None, "gz", "gy", None), P(), P(), P()),
        check_vma=False,
    )
```

```python
import functools

import jax
import jax.numpy as jnp
from jax import lax
from jax.experimental import pallas as pl
from jax.experimental.pallas import tpu as pltpu
from jax.sharding import PartitionSpec as P

OFFSETS = (1, 3, 9)
REACH = 9
BF = jnp.bfloat16
F32 = jnp.float32
PEAK = 1.15e9
PARAMS = pltpu.CompilerParams(vmem_limit_bytes=48 * 1024 * 1024)
VM = pl.BlockSpec(memory_space=pltpu.VMEM)
HELD = pl.BlockSpec(memory_space=pl.ANY)
SM = pl.BlockSpec(memory_space=pltpu.SMEM)


def call(body, outs, args, specs, scratch=(), micros=1.0):
    return pl.pallas_call(
        body,
        out_shape=outs,
        in_specs=specs,
        out_specs=jax.tree.map(lambda _: VM, outs),
        scratch_shapes=list(scratch),
        compiler_params=PARAMS,
        name=getattr(body, "__name__", "final_kernel"),
        cost_estimate=pl.CostEstimate(
            flops=int(micros * PEAK), bytes_accessed=1, transcendentals=0
        ),
    )(*args)


def even_pairs(count):
    return [(i, i ^ 1) for i in range(count - count % 2)]


def odd_pairs(count):
    pairs = [(i, i + 1) for i in range(1, count - 1, 2)]
    return pairs + [(j, i) for i, j in pairs]


def lane_shift(value, step):
    lanes = value.shape[-1]
    moved = pltpu.roll(value, (-step) % lanes, value.ndim - 1)
    lane = lax.broadcasted_iota(jnp.int32, value.shape, value.ndim - 1)
    keep = (lane < lanes - step) if step > 0 else (lane >= -step)
    return jnp.where(keep, moved, 0)


def pair_terms(logits, same):
    target = same.astype(F32)
    small = jnp.exp(-jnp.abs(logits))
    inverse = 1.0 / (1.0 + small)
    sigmoid = jnp.where(logits >= 0, inverse, small * inverse)
    slopes = (sigmoid - target) * 0.25
    losses = jnp.maximum(logits, 0.0) + jnp.log(1.0 + small) - target * logits
    return slopes, losses


def dots(left, right):
    count = left.shape[0]
    parts = []
    for i in range(count):
        part = left[i] * right[i]
        parts.append(part[:8] + part[8:])
    parts += [None] * (-count % 8)
    sub = lax.broadcasted_iota(jnp.int32, parts[0].shape, 0)
    for step in (1, 2, 4):
        own = jnp.bitwise_and(sub, step) == 0
        merged = []
        for first, second in zip(parts[::2], parts[1::2]):
            if first is None:
                merged.append(None)
            elif second is None:
                merged.append(first + pltpu.roll(first, 8 - step, 0))
            else:
                merged.append(
                    jnp.where(own, first, second)
                    + pltpu.roll(jnp.where(own, second, first), 8 - step, 0)
                )
        parts = merged
    return jnp.concatenate(parts, axis=0)[:count] * 0.25


def fill_rim(ext, ye, yo, ze, zo, pz, py, planes, rows):
    ext[1 : planes + 1, (1 - py) * (rows + 1)] = ye[...]
    ext[1 : planes + 1, py * (rows + 1)] = yo[...]
    ext[(1 - pz) * (planes + 1)] = ze[: rows + 2]
    ext[pz * (planes + 1)] = zo[: rows + 2]


def conv_rows(ext, w_ref, z, rows):
    stack = [
        jnp.concatenate([ext[z + a, y + b] for y in rows], axis=1)
        for a in range(3)
        for b in range(3)
    ]
    sums = jnp.dot(w_ref[...], jnp.concatenate(stack, axis=0), preferred_element_type=F32)
    third = sums.shape[0] // 3
    lanes = sums.shape[1] // len(rows)
    for i, y in enumerate(rows):
        part = sums[:, i * lanes : (i + 1) * lanes]
        yield (
            y,
            lane_shift(part[:third], -1)
            + part[third : 2 * third]
            + lane_shift(part[2 * third :], 1),
        )


def pack_labels(wide, blocks):
    at = 0
    for block in blocks:
        count = block.shape[0]
        wide[at : at + count] = lax.shift_right_logical(block, 8).astype(F32)
        wide[at + count : at + 2 * count] = jnp.bitwise_and(block, 255).astype(F32)
        at += 2 * count
    if at < wide.shape[0]:
        wide[at:] = jnp.zeros((wide.shape[0] - at, wide.shape[1]), F32)


def first_kernel(pos, feat, even, odd, sems):
    py, rows = pos[1], feat.shape[1]
    copies = [
        pltpu.make_async_copy(feat.at[:, (1 - py) * (rows - 1)], even, sems.at[0]),
        pltpu.make_async_copy(feat.at[:, py * (rows - 1)], odd, sems.at[1]),
    ]
    for copy in copies:
        copy.start()
    for copy in copies:
        copy.wait()


def second_kernel(pos, feat, lab, w, bias, emb, even, odd, wide):
    planes, rows = feat.shape[0], feat.shape[1]
    py = pos[1]
    cells = (planes - 2) * (REACH - 1)
    for out, high in ((even, 1 - py), (odd, py)):
        pack_labels(
            wide,
            [
                jnp.where(high == 1, lab[z, rows - REACH :], lab[z, :REACH])
                for z in range(planes)
            ],
        )
        out[cells:] = wide[...].astype(BF).reshape(out.shape[0] - cells, *out.shape[1:])

    @pl.loop(0, planes - 2, unroll=True)
    def _(z):
        for y in range(0, rows - 2, 2):
            for i, value in conv_rows(feat, w, z, (y, y + 1)):
                emb[z + 1, i + 1] = (value + bias[...]).astype(BF)

    for out, high in ((even, 1 - py), (odd, py)):
        part = emb[1 : planes - 1, pl.ds(1 + high * (rows - 1 - REACH), REACH - 1)]
        out[:cells] = part.reshape(cells, *part.shape[2:])


def edge_planes(pos, own, ye, yo, even, odd):
    planes, rows = own.shape[0], own.shape[1]
    pz, py = pos[0], pos[1]
    for out, high in ((even, 1 - pz), (odd, pz)):
        plane = high * (planes - 1)
        out[1 : rows + 1] = own[plane]
        out[(1 - py) * (rows + 1)] = ye[plane]
        out[py * (rows + 1)] = yo[plane]


def third_kernel(pos, feat, ye, yo, lab, after, even, odd, wide):
    planes, rows = feat.shape[0], feat.shape[1]
    pz = pos[0]
    edge_planes(pos, feat, ye, yo, even, odd)
    for out, high in ((even, 1 - pz), (odd, pz)):
        base = high * (planes - REACH)
        pack_labels(wide, [lab[base + p] for p in range(REACH)])
        labels = wide[...].astype(BF)
        out[rows + 2 :] = labels.reshape(out.shape[0] - rows - 2, *out.shape[1:])


def forward_kernel(
    pos, part, feat, ye, yo, ze, zo, w, bias, emb, ext, se, so, te, to
):
    planes, rows = emb.shape[0], emb.shape[1]
    pz, py = pos[0], pos[1]
    ext[1 : planes + 1, 1 : rows + 1] = feat[...]
    fill_rim(ext, ye, yo, ze, zo, pz, py, planes, rows)
    emb[1 : planes - 1, 1 : rows - 1] = part[1 : planes - 1, 1 : rows - 1]

    @pl.loop(0, planes, unroll=True)
    def _(z):
        for i, value in conv_rows(ext, w, z, (0, rows - 1)):
            emb[z, i] = (value + bias[...]).astype(BF)

    @pl.loop(0, 2, unroll=True)
    def _(side):
        z = side * (planes - 1)
        for y in range(1, rows - 1, 2):
            for i, value in conv_rows(ext, w, z, (y, y + 1)):
                emb[z, i] = (value + bias[...]).astype(BF)

    for out, high in ((se, 1 - pz), (so, pz)):
        out[...] = emb[pl.ds(high * (planes - REACH), REACH)]
    for out, high in ((te, 1 - py), (to, py)):
        part = pl.ds(high * (rows - REACH), REACH)
        out[:REACH] = emb[0, part]
        out[REACH : 2 * REACH] = emb[planes - 1, part]
        out[2 * REACH :] = emb[1 : planes - 1, high * (rows - 1)]


def inner_kernel(pos, emb, lab, ze, zo, grad, loss, labz, widez):
    planes, rows = emb.shape[0], emb.shape[1]
    lanes = emb.shape[3]
    pz = pos[0]
    for halo, side in ((ze, 1 - pz), (zo, pz)):
        widez[...] = halo[rows + 2 :].reshape(widez.shape).astype(F32)
        for p in range(REACH):
            at = 2 * rows * p
            labz[side, p] = widez[at : at + rows] * 256.0 + widez[at + rows : at + 2 * rows]

    lane = lax.broadcasted_iota(jnp.int32, (rows, lanes), 1)
    loss[...] = jnp.zeros_like(loss)

    @pl.loop(0, planes, unroll=2)
    def _(z):
        center = emb[z].astype(F32)
        here = lab[z]
        total = jnp.zeros(center.shape, F32)
        lost = jnp.zeros((rows, lanes), F32)
        for o in OFFSETS:
            if o < lanes:
                after = pltpu.roll(center, lanes - o, 2)
                before = pltpu.roll(center, o, 2)
                live = lane < lanes - o
                slopes, losses = pair_terms(
                    dots(center, after), here == pltpu.roll(here, lanes - o, 1)
                )
                slopes = jnp.where(live, slopes, 0.0)
                lost = lost + jnp.where(live, losses, 0.0)
                total = total + slopes[:, None, :] * after
                total = total + pltpu.roll(slopes, o, 1)[:, None, :] * before
        grad[z] = total
        for o in OFFSETS:
            if o < rows:
                low, high = center[: rows - o], center[o:]
                slopes, losses = pair_terms(dots(low, high), here[: rows - o] == here[o:])
                grad[z, : rows - o] += slopes[:, None, :] * high
                grad[z, o:] += slopes[:, None, :] * low
                loss[: rows - o] += losses
        loss[:rows] += lost

    for o in OFFSETS:

        @pl.loop(0, planes - o, unroll=True)
        def _(z):
            low, high = emb[z].astype(F32), emb[z + o].astype(F32)
            slopes, losses = pair_terms(dots(low, high), lab[z] == lab[z + o])
            grad[z] += slopes[:, None, :] * high
            grad[z + o] += slopes[:, None, :] * low
            loss[:rows] += losses


def outer_kernel(
    pos,
    emb,
    lab,
    grad_in,
    loss_in,
    ze,
    zo,
    labz,
    fe,
    fo,
    ye,
    yo,
    out,
    shifted,
    ge,
    go,
    sums,
    grad,
    total,
    laby,
    wide,
    halos,
):
    planes, rows = emb.shape[0], emb.shape[1]
    pz, py = pos[0], pos[1]
    third = emb.shape[2]
    cells = (planes - 2) * (REACH - 1)
    grad[...] = grad_in[...]
    total[...] = loss_in[...]
    for halo, side in ((fe, 1 - py), (fo, py)):
        wide[...] = halo[cells:].reshape(wide.shape).astype(F32)
        for z in range(planes):
            at = 2 * REACH * z
            laby[side, z] = wide[at : at + REACH] * 256.0 + wide[at + REACH : at + 2 * REACH]

    for halo, is_high in ((ze, 1 - pz), (zo, pz)):
        weight = (is_high * pos[2]).astype(F32)
        for o in OFFSETS:

            @pl.loop(0, o, unroll=True)
            def _(t):
                p = t + is_high * (planes - o)
                q = t + (1 - is_high) * (REACH - o)
                other = halo[q].astype(F32)
                slopes, losses = pair_terms(
                    dots(emb[p].astype(F32), other),
                    lab[p].astype(F32) == labz[is_high, q],
                )
                grad[p] += slopes[:, None, :] * other
                total[:rows] += losses * weight

    shifted[:, :2] = jnp.zeros((planes, 2) + shifted.shape[2:], BF)
    shifted[:, rows + 2 :] = jnp.zeros((planes, 2) + shifted.shape[2:], BF)
    for early, late, is_high in ((fe, ye, 1 - py), (fo, yo, py)):
        halos[is_high, 0] = late[:REACH]
        halos[is_high, planes - 1] = late[REACH : 2 * REACH]
        halos[is_high, 1 : planes - 1, (1 - is_high) * (REACH - 1)] = late[2 * REACH :]
        part = early[: (planes - 2) * (REACH - 1)]
        halos[is_high, 1 : planes - 1, pl.ds(is_high, REACH - 1)] = part.reshape(
            planes - 2, REACH - 1, *part.shape[1:]
        )
    live = pos[3].astype(F32)

    @pl.loop(0, planes, unroll=True)
    def _(z):
        center = emb[z].astype(F32)
        here = lab[z].astype(F32)
        sum_z = grad[z]
        low = halos[0, z].astype(F32)
        high = halos[1, z].astype(F32)
        lower, upper = [], []
        for o in OFFSETS:
            lower.append((center[:o], low[REACH - o :], here[:o], laby[0, z, REACH - o :]))
            upper.append((center[rows - o :], high[:o], here[rows - o :], laby[1, z, :o]))
        logits = [dots(a, b) for a, b, _, _ in lower + upper]
        mine = jnp.concatenate([c for _, _, c, _ in lower + upper], axis=0)
        theirs = jnp.concatenate([d for _, _, _, d in lower + upper], axis=0)
        slopes, losses = pair_terms(jnp.concatenate(logits, axis=0), mine == theirs)
        half = sum(OFFSETS)
        total[:1] += jnp.sum(losses[half:], axis=0, keepdims=True) * live
        at = 0
        for o, (_, other, _, _) in zip(OFFSETS, lower):
            sum_z = jnp.concatenate(
                [sum_z[:o] + slopes[at : at + o, None, :] * other, sum_z[o:]], axis=0
            )
            at += o
        for o, (_, other, _, _) in zip(OFFSETS, upper):
            sum_z = jnp.concatenate(
                [
                    sum_z[: rows - o],
                    sum_z[rows - o :] + slopes[at : at + o, None, :] * other,
                ],
                axis=0,
            )
            at += o
        value = sum_z.astype(BF)
        out[z] = value
        wide = value.astype(F32)
        shifted[z, 2 : rows + 2, :third] = lane_shift(wide, 1).astype(BF)
        shifted[z, 2 : rows + 2, third : 2 * third] = value
        shifted[z, 2 : rows + 2, 2 * third :] = lane_shift(wide, -1).astype(BF)

    ge[...] = out[:, (1 - py) * (rows - 1)]
    go[...] = out[:, py * (rows - 1)]
    sums[...] = jnp.broadcast_to(jnp.sum(total[...], keepdims=True), sums.shape)


def weight_kernel(shifted, ext, own, lost, out, acc):
    planes, rows = own.shape[0], own.shape[1]
    channels, lanes = own.shape[2], own.shape[3]
    acc[...] = jnp.zeros_like(acc)

    @pl.loop(0, planes, unroll=True)
    def _(z):
        total = acc[...]
        for y in range(0, rows + 2, 2):
            left = jnp.concatenate(
                [
                    jnp.concatenate([shifted[z, y + i + 2 - b] for b in range(3)], axis=0)
                    for i in range(2)
                ],
                axis=1,
            )
            right = jnp.concatenate(
                [
                    jnp.concatenate([ext[z + a, y + i] for a in range(3)], axis=0)
                    for i in range(2)
                ],
                axis=1,
            )
            total = total + lax.dot_general(
                left, right, (((1,), (1,)), ((), ())), preferred_element_type=F32
            )
        acc[...] = total

    height, width = acc.shape
    out[...] = jnp.zeros_like(out)
    out[:height, :width] = acc[...]
    tile = jnp.sum(own[...].astype(F32), axis=(0, 1))
    column = jnp.sum(tile, axis=1, keepdims=True)
    row = lax.broadcasted_iota(jnp.int32, (channels, lanes), 0)
    lane = lax.broadcasted_iota(jnp.int32, (channels, lanes), 1)
    line = jnp.sum(jnp.where(row == lane, column, 0.0), axis=0, keepdims=True)
    first = lax.broadcasted_iota(jnp.int32, (1, lanes), 1)
    out[height : height + 1, :] = jnp.where(first == channels, lost[0:1, :], line)


def backward_kernel(pos, own, ye, yo, ze, zo, w, after, out, ext):
    planes, rows = own.shape[0], own.shape[1]
    ext[1 : planes + 1, 1 : rows + 1] = own[...]
    fill_rim(ext, ye, yo, ze, zo, pos[0], pos[1], planes, rows)

    @pl.loop(0, planes, unroll=True)
    def _(z):
        for y in range(0, rows, 2):
            for i, value in conv_rows(ext, w, z, (y, y + 1)):
                out[z, i] = value.astype(BF)


def spread_kernel(parts, out):
    out[...] = jnp.broadcast_to(jnp.sum(parts[...], axis=0), out.shape)


def final_kernel(voxels, pair_count, total, out, bias, loss):
    groups, channels, width = out.shape
    per = groups // 3
    height = per * channels
    for a in range(3):
        part = total[:height, a * width : (a + 1) * width] * (1.0 / voxels)
        out[a * per : (a + 1) * per] = part.reshape(per, channels, width)
    bias[...] = total[height : height + 1, :channels] * (1.0 / voxels)
    loss[...] = total[height : height + 1, channels : channels + 1] * (1.0 / pair_count)


def per_device(features, labels, weight, conv_bias):
    ch_in, planes, rows, lanes = features.shape
    emb_ch = weight.shape[0]
    gz, gy = lax.axis_size("gz"), lax.axis_size("gy")
    depth, height = planes * gz, rows * gy
    voxels = depth * height * lanes
    pair_count = sum(
        (extent - o) * (voxels // extent)
        for extent in (depth, height, lanes)
        for o in OFFSETS
        if o < extent
    )
    iz, iy = lax.axis_index("gz"), lax.axis_index("gy")
    pos = jnp.stack(
        [
            lax.rem(iz, 2),
            lax.rem(iy, 2),
            (iz < gz - 1).astype(jnp.int32),
            (iy < gy - 1).astype(jnp.int32),
        ]
    ).astype(jnp.int32)
    z_even, z_odd = even_pairs(gz), odd_pairs(gz)
    y_even, y_odd = even_pairs(gy), odd_pairs(gy)

    feat = jnp.transpose(features, (1, 2, 0, 3))
    taps = jnp.transpose(weight, (2, 3, 4, 0, 1))
    w_fwd = jnp.transpose(taps, (2, 3, 0, 1, 4)).reshape(3 * emb_ch, 9 * ch_in)
    w_bwd = jnp.transpose(taps[::-1, ::-1, ::-1], (2, 4, 0, 1, 3)).reshape(
        3 * ch_in, 9 * emb_ch
    )
    bias = jnp.broadcast_to(conv_bias[:, None], (emb_ch, lanes))

    sds = jax.ShapeDtypeStruct
    tile = (emb_ch, lanes)
    cells = (ch_in, lanes)
    z_blocks = -(-2 * REACH * rows // ch_in)
    y_blocks = -(-2 * REACH * planes // ch_in)

    y_message = sds((planes,) + cells, BF)
    me, mo = call(
        first_kernel, (y_message, y_message), (pos, feat), [SM, HELD],
        scratch=[pltpu.SemaphoreType.DMA((2,))],
    )
    fye = lax.ppermute(me, "gy", y_even)
    fyo = lax.ppermute(mo, "gy", y_odd)
    emb_shape = sds((planes, rows) + tile, BF)
    ext_shape = sds((planes + 2, rows + 2) + cells, BF)
    y_early = sds(
        ((planes - 2) * (REACH - 1) + y_blocks * (ch_in // emb_ch),) + tile, BF
    )
    emb_part, me, mo = call(
        second_kernel,
        (emb_shape, y_early, y_early),
        (pos, feat, labels, w_fwd, bias),
        [SM] + [VM] * 4,
        scratch=[pltpu.VMEM((y_blocks * ch_in, lanes), F32)],
        micros=3.4,
    )
    aye = lax.ppermute(me, "gy", y_even)
    ayo = lax.ppermute(mo, "gy", y_odd)
    z_message = sds((rows + 2 + z_blocks,) + cells, BF)
    me, mo = call(
        third_kernel,
        (z_message, z_message),
        (pos, feat, fye, fyo, labels, me),
        [SM] + [VM] * 4 + [HELD],
        scratch=[pltpu.VMEM((z_blocks * ch_in, lanes), F32)],
    )
    fze = lax.ppermute(me, "gz", z_even)
    fzo = lax.ppermute(mo, "gz", z_odd)

    z_halo = sds((REACH, rows) + tile, BF)
    y_late = sds((2 * REACH + planes - 2,) + tile, BF)
    emb, feat_ext, se, so, te, to = call(
        forward_kernel,
        (emb_shape, ext_shape, z_halo, z_halo, y_late, y_late),
        (pos, emb_part, feat, fye, fyo, fze, fzo, w_fwd, bias),
        [SM] + [VM] * 8,
        micros=3.6,
    )
    eze = lax.ppermute(se, "gz", z_even)
    ezo = lax.ppermute(so, "gz", z_odd)
    eye = lax.ppermute(te, "gy", y_even)
    eyo = lax.ppermute(to, "gy", y_odd)

    lost_rows = -(-rows // 8) * 8
    grad_shape = sds((planes, rows) + tile, F32)
    loss_shape = sds((lost_rows, lanes), F32)
    grad_a, loss_a, labz = call(
        inner_kernel,
        (
            grad_shape,
            loss_shape,
            sds((2, REACH, rows, lanes), F32),
        ),
        (pos, emb, labels, fze, fzo),
        [SM] + [VM] * 4,
        scratch=[pltpu.VMEM((z_blocks * ch_in, lanes), F32)],
        micros=6.4,
    )
    grad, shifted, ge, go, lost = call(
        outer_kernel,
        (
            sds((planes, rows) + tile, BF),
            sds((planes, rows + 4, 3 * emb_ch, lanes), BF),
            sds((planes,) + tile, BF),
            sds((planes,) + tile, BF),
            sds((8, lanes), F32),
        ),
        (pos, emb, labels, grad_a, loss_a, eze, ezo, labz, aye, ayo, eye, eyo),
        [SM] + [VM] * 11,
        scratch=[
            pltpu.VMEM((planes, rows) + tile, F32),
            pltpu.VMEM((lost_rows, lanes), F32),
            pltpu.VMEM((2, planes, REACH, lanes), F32),
            pltpu.VMEM((y_blocks * ch_in, lanes), F32),
            pltpu.VMEM((2, planes, REACH) + tile, BF),
        ],
        micros=5.0,
    )
    gye = lax.ppermute(ge, "gy", y_even)
    gyo = lax.ppermute(go, "gy", y_odd)

    used = 9 * emb_ch + 1
    padded = -(-used // (8 * gz)) * 8 * gz
    share = padded // gz
    partial = call(
        weight_kernel,
        sds((padded, lanes), F32),
        (shifted, feat_ext, grad, lost),
        [VM] * 4,
        scratch=[pltpu.VMEM((9 * emb_ch, 3 * ch_in), F32)],
        micros=3.8,
    )
    z_edge = sds((rows + 2,) + tile, BF)
    me, mo = call(edge_planes, (z_edge, z_edge), (pos, grad, gye, gyo), [SM] + [VM] * 3)
    gze = lax.ppermute(me, "gz", z_even)
    gzo = lax.ppermute(mo, "gz", z_odd)

    parts = lax.all_to_all(partial.reshape(gz, share, lanes), "gz", 0, 0)
    mine = call(spread_kernel, sds((gy, share, lanes), F32), (parts,), [VM])
    feature_grad = call(
        backward_kernel,
        sds((planes, rows) + cells, BF),
        (pos, grad, gye, gyo, gze, gzo, w_bwd, mine),
        [SM] + [VM] * 6 + [HELD],
        scratch=[pltpu.VMEM((planes + 2, rows + 2) + tile, BF)],
        micros=4.9,
    )
    parts = lax.all_to_all(mine, "gy", 0, 0)
    mine = call(spread_kernel, sds((gz, share, lanes), F32), (parts,), [VM])
    total = lax.all_to_all(mine, "gz", 0, 0).reshape(padded, lanes)

    weight_grad, bias_grad, loss = call(
        functools.partial(final_kernel, voxels, pair_count),
        (sds((27, emb_ch, ch_in), F32), sds((1, emb_ch), F32), sds((1, 1), F32)),
        (total,),
        [VM],
    )
    weight_grad = jnp.transpose(
        weight_grad.reshape(3, 3, 3, emb_ch, ch_in), (3, 4, 0, 1, 2)
    )
    return (
        jnp.transpose(feature_grad, (2, 0, 1, 3)),
        weight_grad,
        bias_grad.reshape(emb_ch),
        loss.reshape(()),
    )


def solution(mesh):
    return jax.shard_map(
        per_device,
        mesh=mesh,
        in_specs=(P(None, "gz", "gy", None), P("gz", "gy", None), P(), P()),
        out_specs=(P(None, "gz", "gy", None), P(), P(), P()),
        check_vma=False,
    )
```

```python
import functools

import jax
import jax.numpy as jnp
from jax import lax
from jax.experimental import pallas as pl
from jax.experimental.pallas import tpu as pltpu
from jax.sharding import PartitionSpec as P

OFFSETS = (1, 3, 9)
REACH = 9
BF = jnp.bfloat16
F32 = jnp.float32
PEAK = 1.15e9
PARAMS = pltpu.CompilerParams(vmem_limit_bytes=48 * 1024 * 1024)
VM = pl.BlockSpec(memory_space=pltpu.VMEM)
HELD = pl.BlockSpec(memory_space=pl.ANY)
SM = pl.BlockSpec(memory_space=pltpu.SMEM)


def call(body, outs, args, specs, scratch=(), micros=1.0):
    return pl.pallas_call(
        body,
        out_shape=outs,
        in_specs=specs,
        out_specs=jax.tree.map(lambda _: VM, outs),
        scratch_shapes=list(scratch),
        compiler_params=PARAMS,
        name=getattr(body, "__name__", "final_kernel"),
        cost_estimate=pl.CostEstimate(
            flops=int(micros * PEAK), bytes_accessed=1, transcendentals=0
        ),
    )(*args)


def even_pairs(count):
    return [(i, i ^ 1) for i in range(count - count % 2)]


def odd_pairs(count):
    pairs = [(i, i + 1) for i in range(1, count - 1, 2)]
    return pairs + [(j, i) for i, j in pairs]


def lane_shift(value, step):
    lanes = value.shape[-1]
    moved = pltpu.roll(value, (-step) % lanes, value.ndim - 1)
    lane = lax.broadcasted_iota(jnp.int32, value.shape, value.ndim - 1)
    keep = (lane < lanes - step) if step > 0 else (lane >= -step)
    return jnp.where(keep, moved, 0)


def pair_terms(logits, same):
    target = same.astype(F32)
    small = jnp.exp(-jnp.abs(logits))
    inverse = 1.0 / (1.0 + small)
    sigmoid = jnp.where(logits >= 0, inverse, small * inverse)
    slopes = (sigmoid - target) * 0.25
    losses = jnp.maximum(logits, 0.0) + jnp.log(1.0 + small) - target * logits
    return slopes, losses


def dots(left, right):
    count = left.shape[0]
    parts = []
    for i in range(count):
        part = left[i] * right[i]
        parts.append(part[:8] + part[8:])
    parts += [None] * (-count % 8)
    sub = lax.broadcasted_iota(jnp.int32, parts[0].shape, 0)
    for step in (1, 2, 4):
        own = jnp.bitwise_and(sub, step) == 0
        merged = []
        for first, second in zip(parts[::2], parts[1::2]):
            if first is None:
                merged.append(None)
            elif second is None:
                merged.append(first + pltpu.roll(first, 8 - step, 0))
            else:
                merged.append(
                    jnp.where(own, first, second)
                    + pltpu.roll(jnp.where(own, second, first), 8 - step, 0)
                )
        parts = merged
    return jnp.concatenate(parts, axis=0)[:count] * 0.25


def fill_rim(ext, ze, zo, ye, yo, pz, py):
    planes, rows = ext.shape[0] - 2, ext.shape[1] - 2
    ext[(1 - pz) * (planes + 1), 1 : rows + 1] = ze[...]
    ext[pz * (planes + 1), 1 : rows + 1] = zo[...]
    ext[:, (1 - py) * (rows + 1)] = ye[...]
    ext[:, py * (rows + 1)] = yo[...]


def conv_rows(ext, w_ref, z, rows):
    stack = [
        jnp.concatenate([ext[z + a, y + b] for y in rows], axis=1)
        for a in range(3)
        for b in range(3)
    ]
    sums = jnp.dot(w_ref[...], jnp.concatenate(stack, axis=0), preferred_element_type=F32)
    third = sums.shape[0] // 3
    lanes = sums.shape[1] // len(rows)
    for i, y in enumerate(rows):
        part = sums[:, i * lanes : (i + 1) * lanes]
        yield (
            y,
            lane_shift(part[:third], -1)
            + part[third : 2 * third]
            + lane_shift(part[2 * third :], 1),
        )


def pack_labels(wide, blocks):
    at = 0
    for block in blocks:
        count = block.shape[0]
        wide[at : at + count] = lax.shift_right_logical(block, 8).astype(F32)
        wide[at + count : at + 2 * count] = jnp.bitwise_and(block, 255).astype(F32)
        at += 2 * count
    if at < wide.shape[0]:
        wide[at:] = jnp.zeros((wide.shape[0] - at, wide.shape[1]), F32)


def first_kernel(pos, feat, even, odd, sems):
    pz, planes = pos[0], feat.shape[0]
    copies = [
        pltpu.make_async_copy(feat.at[(1 - pz) * (planes - 1)], even, sems.at[0]),
        pltpu.make_async_copy(feat.at[pz * (planes - 1)], odd, sems.at[1]),
    ]
    for copy in copies:
        copy.start()
    for copy in copies:
        copy.wait()


def second_kernel(pos, feat, lab, w, bias, emb, even, odd, lze, lzo, wide, widez):
    planes, rows = feat.shape[0], feat.shape[1]
    pz, py = pos[0], pos[1]
    for out, high in ((lze, 1 - pz), (lzo, pz)):
        base = high * (planes - REACH)
        pack_labels(widez, [lab[base + p] for p in range(REACH)])
        out[...] = widez[...].astype(BF).reshape(out.shape)
    cells = (planes - 2) * (REACH - 1)
    for out, high in ((even, 1 - py), (odd, py)):
        pack_labels(
            wide,
            [
                jnp.where(high == 1, lab[z, rows - REACH :], lab[z, :REACH])
                for z in range(planes)
            ],
        )
        out[cells:] = wide[...].astype(BF).reshape(out.shape[0] - cells, *out.shape[1:])

    @pl.loop(0, planes - 2, unroll=True)
    def _(z):
        for y in range(0, rows - 2, 2):
            for i, value in conv_rows(feat, w, z, (y, y + 1)):
                emb[z + 1, i + 1] = (value + bias[...]).astype(BF)

    for out, high in ((even, 1 - py), (odd, py)):
        part = emb[1 : planes - 1, pl.ds(1 + high * (rows - 1 - REACH), REACH - 1)]
        out[:cells] = part.reshape(cells, *part.shape[2:])


def edge_rows(pos, own, ze, zo, after, even, odd):
    planes, rows = own.shape[0], own.shape[1]
    pz, py = pos[0], pos[1]
    for out, high in ((even, 1 - py), (odd, py)):
        row = high * (rows - 1)
        out[1 : planes + 1] = own[:, row]
        out[(1 - pz) * (planes + 1)] = ze[row]
        out[pz * (planes + 1)] = zo[row]


def forward_kernel(
    pos, part, feat, ze, zo, ye, yo, w, bias, lze, lzo, emb, ext, se, so, te, to
):
    planes, rows = emb.shape[0], emb.shape[1]
    pz, py = pos[0], pos[1]
    ext[1 : planes + 1, 1 : rows + 1] = feat[...]
    fill_rim(ext, ze, zo, ye, yo, pz, py)
    emb[1 : planes - 1, 1 : rows - 1] = part[1 : planes - 1, 1 : rows - 1]

    @pl.loop(0, planes, unroll=True)
    def _(z):
        for i, value in conv_rows(ext, w, z, (0, rows - 1)):
            emb[z, i] = (value + bias[...]).astype(BF)

    @pl.loop(0, 2, unroll=True)
    def _(side):
        z = side * (planes - 1)
        for y in range(1, rows - 1, 2):
            for i, value in conv_rows(ext, w, z, (y, y + 1)):
                emb[z, i] = (value + bias[...]).astype(BF)

    for out, labels, high in ((se, lze, 1 - pz), (so, lzo, pz)):
        halo = emb[pl.ds(high * (planes - REACH), REACH)]
        out[: REACH * rows] = halo.reshape(REACH * rows, *halo.shape[2:])
        out[REACH * rows :] = labels[...]
    for out, high in ((te, 1 - py), (to, py)):
        part = pl.ds(high * (rows - REACH), REACH)
        out[:REACH] = emb[0, part]
        out[REACH : 2 * REACH] = emb[planes - 1, part]
        out[2 * REACH :] = emb[1 : planes - 1, high * (rows - 1)]


def inner_kernel(emb, lab, ae, ao, grad, loss):
    planes, rows = emb.shape[0], emb.shape[1]
    lanes = emb.shape[3]
    lane = lax.broadcasted_iota(jnp.int32, (rows, lanes), 1)
    loss[...] = jnp.zeros_like(loss)

    @pl.loop(0, planes, unroll=2)
    def _(z):
        center = emb[z].astype(F32)
        here = lab[z]
        total = jnp.zeros(center.shape, F32)
        lost = jnp.zeros((rows, lanes), F32)
        for o in OFFSETS:
            if o < lanes:
                after = pltpu.roll(center, lanes - o, 2)
                before = pltpu.roll(center, o, 2)
                live = lane < lanes - o
                slopes, losses = pair_terms(
                    dots(center, after), here == pltpu.roll(here, lanes - o, 1)
                )
                slopes = jnp.where(live, slopes, 0.0)
                lost = lost + jnp.where(live, losses, 0.0)
                total = total + slopes[:, None, :] * after
                total = total + pltpu.roll(slopes, o, 1)[:, None, :] * before
        grad[z] = total
        for o in OFFSETS:
            if o < rows:
                low, high = center[: rows - o], center[o:]
                slopes, losses = pair_terms(dots(low, high), here[: rows - o] == here[o:])
                grad[z, : rows - o] += slopes[:, None, :] * high
                grad[z, o:] += slopes[:, None, :] * low
                loss[: rows - o] += losses
        loss[:rows] += lost

    for o in OFFSETS:

        @pl.loop(0, planes - o, unroll=True)
        def _(z):
            low, high = emb[z].astype(F32), emb[z + o].astype(F32)
            slopes, losses = pair_terms(dots(low, high), lab[z] == lab[z + o])
            grad[z] += slopes[:, None, :] * high
            grad[z + o] += slopes[:, None, :] * low
            loss[:rows] += losses


def outer_kernel(
    pos,
    emb,
    lab,
    grad_in,
    loss_in,
    ze,
    zo,
    fe,
    fo,
    ye,
    yo,
    out,
    shifted,
    ge,
    go,
    sums,
    grad,
    total,
    laby,
    wide,
    halos,
    labz,
    widez,
):
    planes, rows = emb.shape[0], emb.shape[1]
    pz, py = pos[0], pos[1]
    third = emb.shape[2]
    cells = (planes - 2) * (REACH - 1)
    grad[...] = grad_in[...]
    total[...] = loss_in[...]
    for halo, side in ((fe, 1 - py), (fo, py)):
        wide[...] = halo[cells:].reshape(wide.shape).astype(F32)
        for z in range(planes):
            at = 2 * REACH * z
            laby[side, z] = wide[at : at + REACH] * 256.0 + wide[at + REACH : at + 2 * REACH]

    for halo, is_high in ((ze, 1 - pz), (zo, pz)):
        widez[...] = halo[REACH * rows :].reshape(widez.shape).astype(F32)
        for p in range(REACH):
            at = 2 * rows * p
            labz[p] = widez[at : at + rows] * 256.0 + widez[at + rows : at + 2 * rows]
        weight = (is_high * pos[2]).astype(F32)
        for o in OFFSETS:

            @pl.loop(0, o, unroll=True)
            def _(t):
                p = t + is_high * (planes - o)
                q = t + (1 - is_high) * (REACH - o)
                other = halo[pl.ds(q * rows, rows)].astype(F32)
                slopes, losses = pair_terms(
                    dots(emb[p].astype(F32), other),
                    lab[p].astype(F32) == labz[q],
                )
                grad[p] += slopes[:, None, :] * other
                total[:rows] += losses * weight

    shifted[:, :2] = jnp.zeros((planes, 2) + shifted.shape[2:], BF)
    shifted[:, rows + 2 :] = jnp.zeros((planes, 2) + shifted.shape[2:], BF)
    for early, late, is_high in ((fe, ye, 1 - py), (fo, yo, py)):
        halos[is_high, 0] = late[:REACH]
        halos[is_high, planes - 1] = late[REACH : 2 * REACH]
        halos[is_high, 1 : planes - 1, (1 - is_high) * (REACH - 1)] = late[2 * REACH :]
        part = early[: (planes - 2) * (REACH - 1)]
        halos[is_high, 1 : planes - 1, pl.ds(is_high, REACH - 1)] = part.reshape(
            planes - 2, REACH - 1, *part.shape[1:]
        )
    live = pos[3].astype(F32)

    @pl.loop(0, planes, unroll=True)
    def _(z):
        center = emb[z].astype(F32)
        here = lab[z].astype(F32)
        sum_z = grad[z]
        low = halos[0, z].astype(F32)
        high = halos[1, z].astype(F32)
        lower, upper = [], []
        for o in OFFSETS:
            lower.append((center[:o], low[REACH - o :], here[:o], laby[0, z, REACH - o :]))
            upper.append((center[rows - o :], high[:o], here[rows - o :], laby[1, z, :o]))
        logits = [dots(a, b) for a, b, _, _ in lower + upper]
        mine = jnp.concatenate([c for _, _, c, _ in lower + upper], axis=0)
        theirs = jnp.concatenate([d for _, _, _, d in lower + upper], axis=0)
        slopes, losses = pair_terms(jnp.concatenate(logits, axis=0), mine == theirs)
        half = sum(OFFSETS)
        total[:1] += jnp.sum(losses[half:], axis=0, keepdims=True) * live
        at = 0
        for o, (_, other, _, _) in zip(OFFSETS, lower):
            sum_z = jnp.concatenate(
                [sum_z[:o] + slopes[at : at + o, None, :] * other, sum_z[o:]], axis=0
            )
            at += o
        for o, (_, other, _, _) in zip(OFFSETS, upper):
            sum_z = jnp.concatenate(
                [
                    sum_z[: rows - o],
                    sum_z[rows - o :] + slopes[at : at + o, None, :] * other,
                ],
                axis=0,
            )
            at += o
        value = sum_z.astype(BF)
        out[z] = value
        wide = value.astype(F32)
        shifted[z, 2 : rows + 2, :third] = lane_shift(wide, 1).astype(BF)
        shifted[z, 2 : rows + 2, third : 2 * third] = value
        shifted[z, 2 : rows + 2, 2 * third :] = lane_shift(wide, -1).astype(BF)

    ge[...] = out[(1 - pz) * (planes - 1)]
    go[...] = out[pz * (planes - 1)]
    sums[...] = jnp.broadcast_to(jnp.sum(total[...], keepdims=True), sums.shape)


def weight_kernel(shifted, ext, own, lost, out, acc):
    planes, rows = own.shape[0], own.shape[1]
    channels, lanes = own.shape[2], own.shape[3]
    acc[...] = jnp.zeros_like(acc)

    @pl.loop(0, planes, unroll=True)
    def _(z):
        total = acc[...]
        for y in range(0, rows + 2, 2):
            left = jnp.concatenate(
                [
                    jnp.concatenate([shifted[z, y + i + 2 - b] for b in range(3)], axis=0)
                    for i in range(2)
                ],
                axis=1,
            )
            right = jnp.concatenate(
                [
                    jnp.concatenate([ext[z + a, y + i] for a in range(3)], axis=0)
                    for i in range(2)
                ],
                axis=1,
            )
            total = total + lax.dot_general(
                left, right, (((1,), (1,)), ((), ())), preferred_element_type=F32
            )
        acc[...] = total

    height, width = acc.shape
    out[...] = jnp.zeros_like(out)
    out[:height, :width] = acc[...]
    tile = jnp.sum(own[...].astype(F32), axis=(0, 1))
    column = jnp.sum(tile, axis=1, keepdims=True)
    row = lax.broadcasted_iota(jnp.int32, (channels, lanes), 0)
    lane = lax.broadcasted_iota(jnp.int32, (channels, lanes), 1)
    line = jnp.sum(jnp.where(row == lane, column, 0.0), axis=0, keepdims=True)
    first = lax.broadcasted_iota(jnp.int32, (1, lanes), 1)
    out[height : height + 1, :] = jnp.where(first == channels, lost[0:1, :], line)


def backward_kernel(pos, own, ye, yo, ze, zo, w, after, out, ext):
    planes, rows = own.shape[0], own.shape[1]
    ext[1 : planes + 1, 1 : rows + 1] = own[...]
    fill_rim(ext, ze, zo, ye, yo, pos[0], pos[1])

    @pl.loop(0, planes, unroll=True)
    def _(z):
        for y in range(0, rows, 2):
            for i, value in conv_rows(ext, w, z, (y, y + 1)):
                out[z, i] = value.astype(BF)


def spread_kernel(parts, out):
    out[...] = jnp.broadcast_to(jnp.sum(parts[...], axis=0), out.shape)


def final_kernel(voxels, pair_count, total, out, bias, loss):
    groups, channels, width = out.shape
    per = groups // 3
    height = per * channels
    for a in range(3):
        part = total[:height, a * width : (a + 1) * width] * (1.0 / voxels)
        out[a * per : (a + 1) * per] = part.reshape(per, channels, width)
    bias[...] = total[height : height + 1, :channels] * (1.0 / voxels)
    loss[...] = total[height : height + 1, channels : channels + 1] * (1.0 / pair_count)


def per_device(features, labels, weight, conv_bias):
    ch_in, planes, rows, lanes = features.shape
    emb_ch = weight.shape[0]
    gz, gy = lax.axis_size("gz"), lax.axis_size("gy")
    depth, height = planes * gz, rows * gy
    voxels = depth * height * lanes
    pair_count = sum(
        (extent - o) * (voxels // extent)
        for extent in (depth, height, lanes)
        for o in OFFSETS
        if o < extent
    )
    iz, iy = lax.axis_index("gz"), lax.axis_index("gy")
    pos = jnp.stack(
        [
            lax.rem(iz, 2),
            lax.rem(iy, 2),
            (iz < gz - 1).astype(jnp.int32),
            (iy < gy - 1).astype(jnp.int32),
        ]
    ).astype(jnp.int32)
    z_even, z_odd = even_pairs(gz), odd_pairs(gz)
    y_even, y_odd = even_pairs(gy), odd_pairs(gy)

    feat = jnp.transpose(features, (1, 2, 0, 3))
    taps = jnp.transpose(weight, (2, 3, 4, 0, 1))
    w_fwd = jnp.transpose(taps, (2, 3, 0, 1, 4)).reshape(3 * emb_ch, 9 * ch_in)
    w_bwd = jnp.transpose(taps[::-1, ::-1, ::-1], (2, 4, 0, 1, 3)).reshape(
        3 * ch_in, 9 * emb_ch
    )
    bias = jnp.broadcast_to(conv_bias[:, None], (emb_ch, lanes))

    sds = jax.ShapeDtypeStruct
    tile = (emb_ch, lanes)
    cells = (ch_in, lanes)
    z_blocks = -(-2 * REACH * rows // ch_in)
    y_blocks = -(-2 * REACH * planes // ch_in)

    z_message = sds((rows,) + cells, BF)
    me, mo = call(
        first_kernel,
        (z_message, z_message),
        (pos, feat),
        [SM, pl.BlockSpec(memory_space=pltpu.HBM)],
        scratch=[pltpu.SemaphoreType.DMA((2,))],
    )
    fze = lax.ppermute(me, "gz", z_even)
    fzo = lax.ppermute(mo, "gz", z_odd)
    emb_shape = sds((planes, rows) + tile, BF)
    ext_shape = sds((planes + 2, rows + 2) + cells, BF)
    y_early = sds(
        ((planes - 2) * (REACH - 1) + y_blocks * (ch_in // emb_ch),) + tile, BF
    )
    z_labels = sds((z_blocks * (ch_in // emb_ch),) + tile, BF)
    emb_part, me, mo, lze, lzo = call(
        second_kernel,
        (emb_shape, y_early, y_early, z_labels, z_labels),
        (pos, feat, labels, w_fwd, bias),
        [SM] + [VM] * 4,
        scratch=[
            pltpu.VMEM((y_blocks * ch_in, lanes), F32),
            pltpu.VMEM((z_blocks * ch_in, lanes), F32),
        ],
        micros=3.4,
    )
    aye = lax.ppermute(me, "gy", y_even)
    ayo = lax.ppermute(mo, "gy", y_odd)
    y_message = sds((planes + 2,) + cells, BF)
    me, mo = call(
        edge_rows, (y_message, y_message), (pos, feat, fze, fzo, me), [SM] + [VM] * 3 + [HELD]
    )
    fye = lax.ppermute(me, "gy", y_even)
    fyo = lax.ppermute(mo, "gy", y_odd)

    z_halo = sds((REACH * rows + z_labels.shape[0],) + tile, BF)
    y_late = sds((2 * REACH + planes - 2,) + tile, BF)
    emb, feat_ext, se, so, te, to = call(
        forward_kernel,
        (emb_shape, ext_shape, z_halo, z_halo, y_late, y_late),
        (pos, emb_part, feat, fze, fzo, fye, fyo, w_fwd, bias, lze, lzo),
        [SM] + [VM] * 10,
        micros=3.6,
    )
    eze = lax.ppermute(se, "gz", z_even)
    ezo = lax.ppermute(so, "gz", z_odd)
    eye = lax.ppermute(te, "gy", y_even)
    eyo = lax.ppermute(to, "gy", y_odd)

    lost_rows = -(-rows // 8) * 8
    grad_shape = sds((planes, rows) + tile, F32)
    loss_shape = sds((lost_rows, lanes), F32)
    grad_a, loss_a = call(
        inner_kernel,
        (grad_shape, loss_shape),
        (emb, labels, aye, ayo),
        [VM] * 2 + [HELD] * 2,
        micros=4.0,
    )
    grad, shifted, ge, go, lost = call(
        outer_kernel,
        (
            sds((planes, rows) + tile, BF),
            sds((planes, rows + 4, 3 * emb_ch, lanes), BF),
            sds((rows,) + tile, BF),
            sds((rows,) + tile, BF),
            sds((8, lanes), F32),
        ),
        (pos, emb, labels, grad_a, loss_a, eze, ezo, aye, ayo, eye, eyo),
        [SM] + [VM] * 10,
        scratch=[
            pltpu.VMEM((planes, rows) + tile, F32),
            pltpu.VMEM((lost_rows, lanes), F32),
            pltpu.VMEM((2, planes, REACH, lanes), F32),
            pltpu.VMEM((y_blocks * ch_in, lanes), F32),
            pltpu.VMEM((2, planes, REACH) + tile, BF),
            pltpu.VMEM((REACH, rows, lanes), F32),
            pltpu.VMEM((z_blocks * ch_in, lanes), F32),
        ],
        micros=5.0,
    )
    gze = lax.ppermute(ge, "gz", z_even)
    gzo = lax.ppermute(go, "gz", z_odd)

    used = 9 * emb_ch + 1
    padded = -(-used // (8 * gz)) * 8 * gz
    share = padded // gz
    partial = call(
        weight_kernel,
        sds((padded, lanes), F32),
        (shifted, feat_ext, grad, lost),
        [VM] * 4,
        scratch=[pltpu.VMEM((9 * emb_ch, 3 * ch_in), F32)],
        micros=3.8,
    )
    y_edge = sds((planes + 2,) + tile, BF)
    me, mo = call(
        edge_rows, (y_edge, y_edge), (pos, grad, gze, gzo, lost), [SM] + [VM] * 3 + [HELD]
    )
    gye = lax.ppermute(me, "gy", y_even)
    gyo = lax.ppermute(mo, "gy", y_odd)

    parts = lax.all_to_all(partial.reshape(gz, share, lanes), "gz", 0, 0)
    mine = call(spread_kernel, sds((gy, share, lanes), F32), (parts,), [VM])
    feature_grad = call(
        backward_kernel,
        sds((planes, rows) + cells, BF),
        (pos, grad, gye, gyo, gze, gzo, w_bwd, mine),
        [SM] + [VM] * 6 + [HELD],
        scratch=[pltpu.VMEM((planes + 2, rows + 2) + tile, BF)],
        micros=4.9,
    )
    parts = lax.all_to_all(mine, "gy", 0, 0)
    mine = call(spread_kernel, sds((gz, share, lanes), F32), (parts,), [VM])
    total = lax.all_to_all(mine, "gz", 0, 0).reshape(padded, lanes)

    weight_grad, bias_grad, loss = call(
        functools.partial(final_kernel, voxels, pair_count),
        (sds((27, emb_ch, ch_in), F32), sds((1, emb_ch), F32), sds((1, 1), F32)),
        (total,),
        [VM],
    )
    weight_grad = jnp.transpose(
        weight_grad.reshape(3, 3, 3, emb_ch, ch_in), (3, 4, 0, 1, 2)
    )
    return (
        jnp.transpose(feature_grad, (2, 0, 1, 3)),
        weight_grad,
        bias_grad.reshape(emb_ch),
        loss.reshape(()),
    )


def solution(mesh):
    return jax.shard_map(
        per_device,
        mesh=mesh,
        in_specs=(P(None, "gz", "gy", None), P("gz", "gy", None), P(), P()),
        out_specs=(P(None, "gz", "gy", None), P(), P(), P()),
        check_vma=False,
    )
```

```python
import functools

import jax
import jax.numpy as jnp
from jax import lax
from jax.experimental import pallas as pl
from jax.experimental.pallas import tpu as pltpu
from jax.sharding import PartitionSpec as P

OFFSETS = (1, 3, 9)
REACH = 9
BF = jnp.bfloat16
F32 = jnp.float32
PEAK = 1.15e9
PARAMS = pltpu.CompilerParams(vmem_limit_bytes=48 * 1024 * 1024)
VM = pl.BlockSpec(memory_space=pltpu.VMEM)
HELD = pl.BlockSpec(memory_space=pl.ANY)
SM = pl.BlockSpec(memory_space=pltpu.SMEM)


def call(body, outs, args, specs, scratch=(), micros=1.0):
    return pl.pallas_call(
        body,
        out_shape=outs,
        in_specs=specs,
        out_specs=jax.tree.map(lambda _: VM, outs),
        scratch_shapes=list(scratch),
        compiler_params=PARAMS,
        name=getattr(body, "__name__", "final_kernel"),
        cost_estimate=pl.CostEstimate(
            flops=int(micros * PEAK), bytes_accessed=1, transcendentals=0
        ),
    )(*args)


def even_pairs(count):
    return [(i, i ^ 1) for i in range(count - count % 2)]


def odd_pairs(count):
    pairs = [(i, i + 1) for i in range(1, count - 1, 2)]
    return pairs + [(j, i) for i, j in pairs]


def lane_shift(value, step):
    lanes = value.shape[-1]
    moved = pltpu.roll(value, (-step) % lanes, value.ndim - 1)
    lane = lax.broadcasted_iota(jnp.int32, value.shape, value.ndim - 1)
    keep = (lane < lanes - step) if step > 0 else (lane >= -step)
    return jnp.where(keep, moved, 0)


def pair_terms(logits, same):
    target = same.astype(F32)
    small = jnp.exp(-jnp.abs(logits))
    inverse = 1.0 / (1.0 + small)
    sigmoid = jnp.where(logits >= 0, inverse, small * inverse)
    slopes = (sigmoid - target) * 0.25
    losses = jnp.maximum(logits, 0.0) + jnp.log(1.0 + small) - target * logits
    return slopes, losses


def dots(left, right):
    count = left.shape[0]
    parts = []
    for i in range(count):
        part = left[i] * right[i]
        parts.append(part[:8] + part[8:])
    parts += [None] * (-count % 8)
    sub = lax.broadcasted_iota(jnp.int32, parts[0].shape, 0)
    for step in (1, 2, 4):
        own = jnp.bitwise_and(sub, step) == 0
        merged = []
        for first, second in zip(parts[::2], parts[1::2]):
            if first is None:
                merged.append(None)
            elif second is None:
                merged.append(first + pltpu.roll(first, 8 - step, 0))
            else:
                merged.append(
                    jnp.where(own, first, second)
                    + pltpu.roll(jnp.where(own, second, first), 8 - step, 0)
                )
        parts = merged
    return jnp.concatenate(parts, axis=0)[:count] * 0.25


def fill_rim(ext, ze, zo, ye, yo, pz, py):
    planes, rows = ext.shape[0] - 2, ext.shape[1] - 2
    ext[(1 - pz) * (planes + 1), 1 : rows + 1] = ze[...]
    ext[pz * (planes + 1), 1 : rows + 1] = zo[...]
    ext[:, (1 - py) * (rows + 1)] = ye[...]
    ext[:, py * (rows + 1)] = yo[...]


def conv_rows(ext, w_ref, z, rows):
    stack = [
        jnp.concatenate([ext[z + a, y + b] for y in rows], axis=1)
        for a in range(3)
        for b in range(3)
    ]
    sums = jnp.dot(w_ref[...], jnp.concatenate(stack, axis=0), preferred_element_type=F32)
    third = sums.shape[0] // 3
    lanes = sums.shape[1] // len(rows)
    for i, y in enumerate(rows):
        part = sums[:, i * lanes : (i + 1) * lanes]
        yield (
            y,
            lane_shift(part[:third], -1)
            + part[third : 2 * third]
            + lane_shift(part[2 * third :], 1),
        )


def pack_labels(wide, blocks):
    at = 0
    for block in blocks:
        count = block.shape[0]
        wide[at : at + count] = lax.shift_right_logical(block, 8).astype(F32)
        wide[at + count : at + 2 * count] = jnp.bitwise_and(block, 255).astype(F32)
        at += 2 * count
    if at < wide.shape[0]:
        wide[at:] = jnp.zeros((wide.shape[0] - at, wide.shape[1]), F32)


def first_kernel(pos, feat, even, odd, sems):
    pz, planes = pos[0], feat.shape[0]
    copies = [
        pltpu.make_async_copy(feat.at[(1 - pz) * (planes - 1)], even, sems.at[0]),
        pltpu.make_async_copy(feat.at[pz * (planes - 1)], odd, sems.at[1]),
    ]
    for copy in copies:
        copy.start()
    for copy in copies:
        copy.wait()


def second_kernel(pos, feat, lab, w, bias, emb, even, odd, lze, lzo, wide, widez):
    planes, rows = feat.shape[0], feat.shape[1]
    pz, py = pos[0], pos[1]
    for out, high in ((lze, 1 - pz), (lzo, pz)):
        base = high * (planes - REACH)
        pack_labels(widez, [lab[base + p] for p in range(REACH)])
        out[...] = widez[...].astype(BF).reshape(out.shape)
    cells = (planes - 2) * (REACH - 1)
    for out, high in ((even, 1 - py), (odd, py)):
        pack_labels(
            wide,
            [
                jnp.where(high == 1, lab[z, rows - REACH :], lab[z, :REACH])
                for z in range(planes)
            ],
        )
        out[cells:] = wide[...].astype(BF).reshape(out.shape[0] - cells, *out.shape[1:])

    @pl.loop(0, planes - 2, unroll=True)
    def _(z):
        for y in range(0, rows - 2, 2):
            for i, value in conv_rows(feat, w, z, (y, y + 1)):
                emb[z + 1, i + 1] = (value + bias[...]).astype(BF)

    for out, high in ((even, 1 - py), (odd, py)):
        part = emb[1 : planes - 1, pl.ds(1 + high * (rows - 1 - REACH), REACH - 1)]
        out[:cells] = part.reshape(cells, *part.shape[2:])


def edge_rows(pos, own, ze, zo, after, even, odd):
    planes, rows = own.shape[0], own.shape[1]
    pz, py = pos[0], pos[1]
    for out, high in ((even, 1 - py), (odd, py)):
        row = high * (rows - 1)
        out[1 : planes + 1] = own[:, row]
        out[(1 - pz) * (planes + 1)] = ze[row]
        out[pz * (planes + 1)] = zo[row]


def forward_kernel(
    pos, part, feat, ze, zo, ye, yo, w, bias, lze, lzo, emb, ext, se, so, te, to
):
    planes, rows = emb.shape[0], emb.shape[1]
    pz, py = pos[0], pos[1]
    ext[1 : planes + 1, 1 : rows + 1] = feat[...]
    fill_rim(ext, ze, zo, ye, yo, pz, py)
    emb[1 : planes - 1, 1 : rows - 1] = part[1 : planes - 1, 1 : rows - 1]

    @pl.loop(0, planes, unroll=True)
    def _(z):
        for i, value in conv_rows(ext, w, z, (0, rows - 1)):
            emb[z, i] = (value + bias[...]).astype(BF)

    @pl.loop(0, 2, unroll=True)
    def _(side):
        z = side * (planes - 1)
        for y in range(1, rows - 1, 2):
            for i, value in conv_rows(ext, w, z, (y, y + 1)):
                emb[z, i] = (value + bias[...]).astype(BF)

    for out, labels, high in ((se, lze, 1 - pz), (so, lzo, pz)):
        halo = emb[pl.ds(high * (planes - REACH), REACH)]
        out[: REACH * rows] = halo.reshape(REACH * rows, *halo.shape[2:])
        out[REACH * rows :] = labels[...]
    for out, high in ((te, 1 - py), (to, py)):
        part = pl.ds(high * (rows - REACH), REACH)
        out[:REACH] = emb[0, part]
        out[REACH : 2 * REACH] = emb[planes - 1, part]
        out[2 * REACH :] = emb[1 : planes - 1, high * (rows - 1)]


def inner_kernel(emb, lab, ae, ao, grad, loss):
    planes, rows = emb.shape[0], emb.shape[1]
    lanes = emb.shape[3]
    lane = lax.broadcasted_iota(jnp.int32, (rows, lanes), 1)
    loss[...] = jnp.zeros_like(loss)

    @pl.loop(0, planes, unroll=2)
    def _(z):
        center = emb[z].astype(F32)
        here = lab[z]
        total = jnp.zeros(center.shape, F32)
        lost = jnp.zeros((rows, lanes), F32)
        for o in OFFSETS:
            if o < lanes:
                after = pltpu.roll(center, lanes - o, 2)
                before = pltpu.roll(center, o, 2)
                live = lane < lanes - o
                slopes, losses = pair_terms(
                    dots(center, after), here == pltpu.roll(here, lanes - o, 1)
                )
                slopes = jnp.where(live, slopes, 0.0)
                lost = lost + jnp.where(live, losses, 0.0)
                total = total + slopes[:, None, :] * after
                total = total + pltpu.roll(slopes, o, 1)[:, None, :] * before
        grad[z] = total
        for o in OFFSETS:
            if o < rows:
                low, high = center[: rows - o], center[o:]
                slopes, losses = pair_terms(dots(low, high), here[: rows - o] == here[o:])
                grad[z, : rows - o] += slopes[:, None, :] * high
                grad[z, o:] += slopes[:, None, :] * low
                loss[: rows - o] += losses
        loss[:rows] += lost

    for o in OFFSETS:

        @pl.loop(0, planes - o, unroll=True)
        def _(z):
            low, high = emb[z].astype(F32), emb[z + o].astype(F32)
            slopes, losses = pair_terms(dots(low, high), lab[z] == lab[z + o])
            grad[z] += slopes[:, None, :] * high
            grad[z + o] += slopes[:, None, :] * low
            loss[:rows] += losses


def outer_z_kernel(pos, emb, lab, grad_in, loss_in, ze, zo, grad, total, labz, widez):
    planes, rows = emb.shape[0], emb.shape[1]
    pz = pos[0]
    grad[...] = grad_in[...]
    total[...] = loss_in[...]
    for halo, is_high in ((ze, 1 - pz), (zo, pz)):
        widez[...] = halo[REACH * rows :].reshape(widez.shape).astype(F32)
        for p in range(REACH):
            at = 2 * rows * p
            labz[p] = widez[at : at + rows] * 256.0 + widez[at + rows : at + 2 * rows]
        weight = (is_high * pos[2]).astype(F32)
        for o in OFFSETS:

            @pl.loop(0, o, unroll=True)
            def _(t):
                p = t + is_high * (planes - o)
                q = t + (1 - is_high) * (REACH - o)
                other = halo[pl.ds(q * rows, rows)].astype(F32)
                slopes, losses = pair_terms(
                    dots(emb[p].astype(F32), other),
                    lab[p].astype(F32) == labz[q],
                )
                grad[p] += slopes[:, None, :] * other
                total[:rows] += losses * weight


def outer_kernel(
    pos,
    emb,
    lab,
    grad,
    loss_in,
    fe,
    fo,
    ye,
    yo,
    ext,
    out,
    ge,
    go,
    packed,
    shifted,
    total,
    laby,
    wide,
    halos,
    acc,
):
    planes, rows = emb.shape[0], emb.shape[1]
    pz, py = pos[0], pos[1]
    channels, lanes = emb.shape[2], emb.shape[3]
    third = channels
    cells = (planes - 2) * (REACH - 1)
    total[...] = loss_in[...]
    for halo, side in ((fe, 1 - py), (fo, py)):
        wide[...] = halo[cells:].reshape(wide.shape).astype(F32)
        for z in range(planes):
            at = 2 * REACH * z
            laby[side, z] = wide[at : at + REACH] * 256.0 + wide[at + REACH : at + 2 * REACH]

    shifted[:, :2] = jnp.zeros((planes, 2) + shifted.shape[2:], BF)
    shifted[:, rows + 2 :] = jnp.zeros((planes, 2) + shifted.shape[2:], BF)
    for early, late, is_high in ((fe, ye, 1 - py), (fo, yo, py)):
        halos[is_high, 0] = late[:REACH]
        halos[is_high, planes - 1] = late[REACH : 2 * REACH]
        halos[is_high, 1 : planes - 1, (1 - is_high) * (REACH - 1)] = late[2 * REACH :]
        part = early[: (planes - 2) * (REACH - 1)]
        halos[is_high, 1 : planes - 1, pl.ds(is_high, REACH - 1)] = part.reshape(
            planes - 2, REACH - 1, *part.shape[1:]
        )
    live = pos[3].astype(F32)

    @pl.loop(0, planes, unroll=True)
    def _(z):
        center = emb[z].astype(F32)
        here = lab[z].astype(F32)
        sum_z = grad[z]
        low = halos[0, z].astype(F32)
        high = halos[1, z].astype(F32)
        lower, upper = [], []
        for o in OFFSETS:
            lower.append((center[:o], low[REACH - o :], here[:o], laby[0, z, REACH - o :]))
            upper.append((center[rows - o :], high[:o], here[rows - o :], laby[1, z, :o]))
        logits = [dots(a, b) for a, b, _, _ in lower + upper]
        mine = jnp.concatenate([c for _, _, c, _ in lower + upper], axis=0)
        theirs = jnp.concatenate([d for _, _, _, d in lower + upper], axis=0)
        slopes, losses = pair_terms(jnp.concatenate(logits, axis=0), mine == theirs)
        half = sum(OFFSETS)
        total[:1] += jnp.sum(losses[half:], axis=0, keepdims=True) * live
        at = 0
        for o, (_, other, _, _) in zip(OFFSETS, lower):
            sum_z = jnp.concatenate(
                [sum_z[:o] + slopes[at : at + o, None, :] * other, sum_z[o:]], axis=0
            )
            at += o
        for o, (_, other, _, _) in zip(OFFSETS, upper):
            sum_z = jnp.concatenate(
                [
                    sum_z[: rows - o],
                    sum_z[rows - o :] + slopes[at : at + o, None, :] * other,
                ],
                axis=0,
            )
            at += o
        value = sum_z.astype(BF)
        out[z] = value
        wide = value.astype(F32)
        shifted[z, 2 : rows + 2, :third] = lane_shift(wide, 1).astype(BF)
        shifted[z, 2 : rows + 2, third : 2 * third] = value
        shifted[z, 2 : rows + 2, 2 * third :] = lane_shift(wide, -1).astype(BF)

    ge[...] = out[(1 - pz) * (planes - 1)]
    go[...] = out[pz * (planes - 1)]

    acc[...] = jnp.zeros_like(acc)

    @pl.loop(0, planes, unroll=True)
    def _(z):
        products = acc[...]
        for y in range(0, rows + 2, 2):
            left = jnp.concatenate(
                [
                    jnp.concatenate([shifted[z, y + i + 2 - b] for b in range(3)], axis=0)
                    for i in range(2)
                ],
                axis=1,
            )
            right = jnp.concatenate(
                [
                    jnp.concatenate([ext[z + a, y + i] for a in range(3)], axis=0)
                    for i in range(2)
                ],
                axis=1,
            )
            products = products + lax.dot_general(
                left, right, (((1,), (1,)), ((), ())), preferred_element_type=F32
            )
        acc[...] = products

    height, width = acc.shape
    packed[...] = jnp.zeros_like(packed)
    packed[:height, :width] = acc[...]
    tile = jnp.sum(out[...].astype(F32), axis=(0, 1))
    column = jnp.sum(tile, axis=1, keepdims=True)
    row = lax.broadcasted_iota(jnp.int32, (channels, lanes), 0)
    lane = lax.broadcasted_iota(jnp.int32, (channels, lanes), 1)
    line = jnp.sum(jnp.where(row == lane, column, 0.0), axis=0, keepdims=True)
    first = lax.broadcasted_iota(jnp.int32, (1, lanes), 1)
    packed[height : height + 1, :] = jnp.where(first == channels, jnp.sum(total[...], keepdims=True), line)


def backward_kernel(pos, own, ye, yo, ze, zo, w, after, out, ext):
    planes, rows = own.shape[0], own.shape[1]
    ext[1 : planes + 1, 1 : rows + 1] = own[...]
    fill_rim(ext, ze, zo, ye, yo, pos[0], pos[1])

    @pl.loop(0, planes, unroll=True)
    def _(z):
        for y in range(0, rows, 2):
            for i, value in conv_rows(ext, w, z, (y, y + 1)):
                out[z, i] = value.astype(BF)


def spread_kernel(parts, out):
    out[...] = jnp.broadcast_to(jnp.sum(parts[...], axis=0), out.shape)


def final_kernel(voxels, pair_count, total, out, bias, loss):
    groups, channels, width = out.shape
    per = groups // 3
    height = per * channels
    for a in range(3):
        part = total[:height, a * width : (a + 1) * width] * (1.0 / voxels)
        out[a * per : (a + 1) * per] = part.reshape(per, channels, width)
    bias[...] = total[height : height + 1, :channels] * (1.0 / voxels)
    loss[...] = total[height : height + 1, channels : channels + 1] * (1.0 / pair_count)


def per_device(features, labels, weight, conv_bias):
    ch_in, planes, rows, lanes = features.shape
    emb_ch = weight.shape[0]
    gz, gy = lax.axis_size("gz"), lax.axis_size("gy")
    depth, height = planes * gz, rows * gy
    voxels = depth * height * lanes
    pair_count = sum(
        (extent - o) * (voxels // extent)
        for extent in (depth, height, lanes)
        for o in OFFSETS
        if o < extent
    )
    iz, iy = lax.axis_index("gz"), lax.axis_index("gy")
    pos = jnp.stack(
        [
            lax.rem(iz, 2),
            lax.rem(iy, 2),
            (iz < gz - 1).astype(jnp.int32),
            (iy < gy - 1).astype(jnp.int32),
        ]
    ).astype(jnp.int32)
    z_even, z_odd = even_pairs(gz), odd_pairs(gz)
    y_even, y_odd = even_pairs(gy), odd_pairs(gy)

    feat = jnp.transpose(features, (1, 2, 0, 3))
    taps = jnp.transpose(weight, (2, 3, 4, 0, 1))
    w_fwd = jnp.transpose(taps, (2, 3, 0, 1, 4)).reshape(3 * emb_ch, 9 * ch_in)
    w_bwd = jnp.transpose(taps[::-1, ::-1, ::-1], (2, 4, 0, 1, 3)).reshape(
        3 * ch_in, 9 * emb_ch
    )
    bias = jnp.broadcast_to(conv_bias[:, None], (emb_ch, lanes))

    sds = jax.ShapeDtypeStruct
    tile = (emb_ch, lanes)
    cells = (ch_in, lanes)
    z_blocks = -(-2 * REACH * rows // ch_in)
    y_blocks = -(-2 * REACH * planes // ch_in)

    z_message = sds((rows,) + cells, BF)
    me, mo = call(
        first_kernel,
        (z_message, z_message),
        (pos, feat),
        [SM, pl.BlockSpec(memory_space=pltpu.HBM)],
        scratch=[pltpu.SemaphoreType.DMA((2,))],
    )
    fze = lax.ppermute(me, "gz", z_even)
    fzo = lax.ppermute(mo, "gz", z_odd)
    emb_shape = sds((planes, rows) + tile, BF)
    ext_shape = sds((planes + 2, rows + 2) + cells, BF)
    y_early = sds(
        ((planes - 2) * (REACH - 1) + y_blocks * (ch_in // emb_ch),) + tile, BF
    )
    z_labels = sds((z_blocks * (ch_in // emb_ch),) + tile, BF)
    emb_part, me, mo, lze, lzo = call(
        second_kernel,
        (emb_shape, y_early, y_early, z_labels, z_labels),
        (pos, feat, labels, w_fwd, bias),
        [SM] + [VM] * 4,
        scratch=[
            pltpu.VMEM((y_blocks * ch_in, lanes), F32),
            pltpu.VMEM((z_blocks * ch_in, lanes), F32),
        ],
        micros=3.4,
    )
    aye = lax.ppermute(me, "gy", y_even)
    ayo = lax.ppermute(mo, "gy", y_odd)
    y_message = sds((planes + 2,) + cells, BF)
    me, mo = call(
        edge_rows, (y_message, y_message), (pos, feat, fze, fzo, me), [SM] + [VM] * 3 + [HELD]
    )
    fye = lax.ppermute(me, "gy", y_even)
    fyo = lax.ppermute(mo, "gy", y_odd)

    z_halo = sds((REACH * rows + z_labels.shape[0],) + tile, BF)
    y_late = sds((2 * REACH + planes - 2,) + tile, BF)
    emb, feat_ext, se, so, te, to = call(
        forward_kernel,
        (emb_shape, ext_shape, z_halo, z_halo, y_late, y_late),
        (pos, emb_part, feat, fze, fzo, fye, fyo, w_fwd, bias, lze, lzo),
        [SM] + [VM] * 10,
        micros=3.6,
    )
    eze = lax.ppermute(se, "gz", z_even)
    ezo = lax.ppermute(so, "gz", z_odd)
    eye = lax.ppermute(te, "gy", y_even)
    eyo = lax.ppermute(to, "gy", y_odd)

    lost_rows = -(-rows // 8) * 8
    grad_shape = sds((planes, rows) + tile, F32)
    loss_shape = sds((lost_rows, lanes), F32)
    grad_a, loss_a = call(
        inner_kernel,
        (grad_shape, loss_shape),
        (emb, labels, aye, ayo),
        [VM] * 2 + [HELD] * 2,
        micros=4.0,
    )
    grad_b, loss_b = call(
        outer_z_kernel,
        (grad_shape, loss_shape),
        (pos, emb, labels, grad_a, loss_a, eze, ezo),
        [SM] + [VM] * 6,
        scratch=[
            pltpu.VMEM((REACH, rows, lanes), F32),
            pltpu.VMEM((z_blocks * ch_in, lanes), F32),
        ],
        micros=1.5,
    )
    used = 9 * emb_ch + 1
    padded = -(-used // (8 * gz)) * 8 * gz
    share = padded // gz
    grad, ge, go, partial = call(
        outer_kernel,
        (
            sds((planes, rows) + tile, BF),
            sds((rows,) + tile, BF),
            sds((rows,) + tile, BF),
            sds((padded, lanes), F32),
        ),
        (pos, emb, labels, grad_b, loss_b, aye, ayo, eye, eyo, feat_ext),
        [SM] + [VM] * 9,
        scratch=[
            pltpu.VMEM((planes, rows + 4, 3 * emb_ch, lanes), BF),
            pltpu.VMEM((lost_rows, lanes), F32),
            pltpu.VMEM((2, planes, REACH, lanes), F32),
            pltpu.VMEM((y_blocks * ch_in, lanes), F32),
            pltpu.VMEM((2, planes, REACH) + tile, BF),
            pltpu.VMEM((9 * emb_ch, 3 * ch_in), F32),
        ],
        micros=3.7,
    )
    gze = lax.ppermute(ge, "gz", z_even)
    gzo = lax.ppermute(go, "gz", z_odd)

    y_edge = sds((planes + 2,) + tile, BF)
    me, mo = call(
        edge_rows, (y_edge, y_edge), (pos, grad, gze, gzo, ge), [SM] + [VM] * 3 + [HELD]
    )
    gye = lax.ppermute(me, "gy", y_even)
    gyo = lax.ppermute(mo, "gy", y_odd)

    parts = lax.all_to_all(partial.reshape(gz, share, lanes), "gz", 0, 0)
    mine = call(spread_kernel, sds((gy, share, lanes), F32), (parts,), [VM])
    feature_grad = call(
        backward_kernel,
        sds((planes, rows) + cells, BF),
        (pos, grad, gye, gyo, gze, gzo, w_bwd, mine),
        [SM] + [VM] * 6 + [HELD],
        scratch=[pltpu.VMEM((planes + 2, rows + 2) + tile, BF)],
        micros=4.9,
    )
    parts = lax.all_to_all(mine, "gy", 0, 0)
    mine = call(spread_kernel, sds((gz, share, lanes), F32), (parts,), [VM])
    total = lax.all_to_all(mine, "gz", 0, 0).reshape(padded, lanes)

    weight_grad, bias_grad, loss = call(
        functools.partial(final_kernel, voxels, pair_count),
        (sds((27, emb_ch, ch_in), F32), sds((1, emb_ch), F32), sds((1, 1), F32)),
        (total,),
        [VM],
    )
    weight_grad = jnp.transpose(
        weight_grad.reshape(3, 3, 3, emb_ch, ch_in), (3, 4, 0, 1, 2)
    )
    return (
        jnp.transpose(feature_grad, (2, 0, 1, 3)),
        weight_grad,
        bias_grad.reshape(emb_ch),
        loss.reshape(()),
    )


def solution(mesh):
    return jax.shard_map(
        per_device,
        mesh=mesh,
        in_specs=(P(None, "gz", "gy", None), P("gz", "gy", None), P(), P()),
        out_specs=(P(None, "gz", "gy", None), P(), P(), P()),
        check_vma=False,
    )
```

```python
import functools

import jax
import jax.numpy as jnp
from jax import lax
from jax.experimental import pallas as pl
from jax.experimental.pallas import tpu as pltpu
from jax.sharding import PartitionSpec as P

OFFSETS = (1, 3, 9)
REACH = 9
BF = jnp.bfloat16
F32 = jnp.float32
PEAK = 1.15e9
PARAMS = pltpu.CompilerParams(vmem_limit_bytes=48 * 1024 * 1024)
VM = pl.BlockSpec(memory_space=pltpu.VMEM)
HELD = pl.BlockSpec(memory_space=pl.ANY)
SM = pl.BlockSpec(memory_space=pltpu.SMEM)


def call(body, outs, args, specs, scratch=(), micros=1.0):
    return pl.pallas_call(
        body,
        out_shape=outs,
        in_specs=specs,
        out_specs=jax.tree.map(lambda _: VM, outs),
        scratch_shapes=list(scratch),
        compiler_params=PARAMS,
        name=getattr(body, "__name__", "final_kernel"),
        cost_estimate=pl.CostEstimate(
            flops=int(micros * PEAK), bytes_accessed=1, transcendentals=0
        ),
    )(*args)


def even_pairs(count):
    return [(i, i ^ 1) for i in range(count - count % 2)]


def odd_pairs(count):
    pairs = [(i, i + 1) for i in range(1, count - 1, 2)]
    return pairs + [(j, i) for i, j in pairs]


def lane_shift(value, step):
    lanes = value.shape[-1]
    moved = pltpu.roll(value, (-step) % lanes, value.ndim - 1)
    lane = lax.broadcasted_iota(jnp.int32, value.shape, value.ndim - 1)
    keep = (lane < lanes - step) if step > 0 else (lane >= -step)
    return jnp.where(keep, moved, 0)


def pair_terms(logits, same):
    target = same.astype(F32)
    small = jnp.exp(-jnp.abs(logits))
    inverse = 1.0 / (1.0 + small)
    sigmoid = jnp.where(logits >= 0, inverse, small * inverse)
    slopes = (sigmoid - target) * 0.25
    losses = jnp.maximum(logits, 0.0) + jnp.log1p(small) - target * logits
    return slopes, losses


def dots(left, right):
    count = left.shape[0]
    parts = []
    for i in range(count):
        part = left[i] * right[i]
        parts.append(part[:8] + part[8:])
    parts += [None] * (-count % 8)
    sub = lax.broadcasted_iota(jnp.int32, parts[0].shape, 0)
    for step in (1, 2, 4):
        own = jnp.bitwise_and(sub, step) == 0
        merged = []
        for first, second in zip(parts[::2], parts[1::2]):
            if first is None:
                merged.append(None)
            elif second is None:
                merged.append(first + pltpu.roll(first, 8 - step, 0))
            else:
                merged.append(
                    jnp.where(own, first, second)
                    + pltpu.roll(jnp.where(own, second, first), 8 - step, 0)
                )
        parts = merged
    return jnp.concatenate(parts, axis=0)[:count] * 0.25


def fill_rim(ext, ze, zo, ye, yo, pz, py):
    planes, rows = ext.shape[0] - 2, ext.shape[1] - 2
    ext[(1 - pz) * (planes + 1), 1 : rows + 1] = ze[...]
    ext[pz * (planes + 1), 1 : rows + 1] = zo[...]
    ext[:, (1 - py) * (rows + 1)] = ye[...]
    ext[:, py * (rows + 1)] = yo[...]


def conv_rows(ext, w_ref, z, rows):
    stack = [
        jnp.concatenate([ext[z + a, y + b] for y in rows], axis=1)
        for a in range(3)
        for b in range(3)
    ]
    sums = jnp.dot(w_ref[...], jnp.concatenate(stack, axis=0), preferred_element_type=F32)
    third = sums.shape[0] // 3
    lanes = sums.shape[1] // len(rows)
    for i, y in enumerate(rows):
        part = sums[:, i * lanes : (i + 1) * lanes]
        yield (
            y,
            lane_shift(part[:third], -1)
            + part[third : 2 * third]
            + lane_shift(part[2 * third :], 1),
        )


def pack_labels(wide, blocks):
    at = 0
    for block in blocks:
        count = block.shape[0]
        wide[at : at + count] = lax.shift_right_logical(block, 8).astype(F32)
        wide[at + count : at + 2 * count] = jnp.bitwise_and(block, 255).astype(F32)
        at += 2 * count
    if at < wide.shape[0]:
        wide[at:] = jnp.zeros((wide.shape[0] - at, wide.shape[1]), F32)


def first_kernel(pos, feat, even, odd, sems):
    pz, planes = pos[0], feat.shape[0]
    copies = [
        pltpu.make_async_copy(feat.at[(1 - pz) * (planes - 1)], even, sems.at[0]),
        pltpu.make_async_copy(feat.at[pz * (planes - 1)], odd, sems.at[1]),
    ]
    for copy in copies:
        copy.start()
    for copy in copies:
        copy.wait()


def second_kernel(pos, feat, lab, w, bias, emb, even, odd, lze, lzo, wide, widez):
    planes, rows = feat.shape[0], feat.shape[1]
    pz, py = pos[0], pos[1]
    for out, high in ((lze, 1 - pz), (lzo, pz)):
        base = high * (planes - REACH)
        pack_labels(widez, [lab[base + p] for p in range(REACH)])
        out[...] = widez[...].astype(BF).reshape(out.shape)
    cells = (planes - 2) * (REACH - 1)
    for out, high in ((even, 1 - py), (odd, py)):
        pack_labels(
            wide,
            [
                jnp.where(high == 1, lab[z, rows - REACH :], lab[z, :REACH])
                for z in range(planes)
            ],
        )
        out[cells:] = wide[...].astype(BF).reshape(out.shape[0] - cells, *out.shape[1:])

    @pl.loop(0, planes - 2, unroll=True)
    def _(z):
        for y in range(0, rows - 2, 2):
            for i, value in conv_rows(feat, w, z, (y, y + 1)):
                emb[z + 1, i + 1] = (value + bias[...]).astype(BF)

    for out, high in ((even, 1 - py), (odd, py)):
        part = emb[1 : planes - 1, pl.ds(1 + high * (rows - 1 - REACH), REACH - 1)]
        out[:cells] = part.reshape(cells, *part.shape[2:])


def edge_rows(pos, own, ze, zo, after, even, odd):
    planes, rows = own.shape[0], own.shape[1]
    pz, py = pos[0], pos[1]
    for out, high in ((even, 1 - py), (odd, py)):
        row = high * (rows - 1)
        out[1 : planes + 1] = own[:, row]
        out[(1 - pz) * (planes + 1)] = ze[row]
        out[pz * (planes + 1)] = zo[row]


def forward_kernel(
    pos, part, feat, ze, zo, ye, yo, w, bias, lze, lzo, emb, ext, se, so, te, to
):
    planes, rows = emb.shape[0], emb.shape[1]
    pz, py = pos[0], pos[1]
    ext[1 : planes + 1, 1 : rows + 1] = feat[...]
    fill_rim(ext, ze, zo, ye, yo, pz, py)
    emb[1 : planes - 1, 1 : rows - 1] = part[1 : planes - 1, 1 : rows - 1]

    @pl.loop(0, planes, unroll=True)
    def _(z):
        for i, value in conv_rows(ext, w, z, (0, rows - 1)):
            emb[z, i] = (value + bias[...]).astype(BF)

    @pl.loop(0, 2, unroll=True)
    def _(side):
        z = side * (planes - 1)
        for y in range(1, rows - 1, 2):
            for i, value in conv_rows(ext, w, z, (y, y + 1)):
                emb[z, i] = (value + bias[...]).astype(BF)

    for out, labels, high in ((se, lze, 1 - pz), (so, lzo, pz)):
        halo = emb[pl.ds(high * (planes - REACH), REACH)]
        out[: REACH * rows] = halo.reshape(REACH * rows, *halo.shape[2:])
        out[REACH * rows :] = labels[...]
    for out, high in ((te, 1 - py), (to, py)):
        part = pl.ds(high * (rows - REACH), REACH)
        out[:REACH] = emb[0, part]
        out[REACH : 2 * REACH] = emb[planes - 1, part]
        out[2 * REACH :] = emb[1 : planes - 1, high * (rows - 1)]


def inner_kernel(emb, lab, ae, ao, grad, loss):
    planes, rows = emb.shape[0], emb.shape[1]
    lanes = emb.shape[3]
    lane = lax.broadcasted_iota(jnp.int32, (rows, lanes), 1)
    loss[...] = jnp.zeros_like(loss)

    @pl.loop(0, planes, unroll=2)
    def _(z):
        center = emb[z].astype(F32)
        here = lab[z]
        total = jnp.zeros(center.shape, F32)
        lost = jnp.zeros((rows, lanes), F32)
        for o in OFFSETS:
            if o < lanes:
                after = pltpu.roll(center, lanes - o, 2)
                before = pltpu.roll(center, o, 2)
                live = lane < lanes - o
                slopes, losses = pair_terms(
                    dots(center, after), here == pltpu.roll(here, lanes - o, 1)
                )
                slopes = jnp.where(live, slopes, 0.0)
                lost = lost + jnp.where(live, losses, 0.0)
                total = total + slopes[:, None, :] * after
                total = total + pltpu.roll(slopes, o, 1)[:, None, :] * before
        grad[z] = total
        for o in OFFSETS:
            if o < rows:
                low, high = center[: rows - o], center[o:]
                slopes, losses = pair_terms(dots(low, high), here[: rows - o] == here[o:])
                grad[z, : rows - o] += slopes[:, None, :] * high
                grad[z, o:] += slopes[:, None, :] * low
                loss[: rows - o] += losses
        loss[:rows] += lost

    for o in OFFSETS:

        @pl.loop(0, planes - o, unroll=True)
        def _(z):
            low, high = emb[z].astype(F32), emb[z + o].astype(F32)
            slopes, losses = pair_terms(dots(low, high), lab[z] == lab[z + o])
            grad[z] += slopes[:, None, :] * high
            grad[z + o] += slopes[:, None, :] * low
            loss[:rows] += losses


def outer_z_kernel(pos, emb, lab, grad_in, loss_in, ze, zo, grad, total, labz, widez):
    planes, rows = emb.shape[0], emb.shape[1]
    pz = pos[0]
    grad[...] = grad_in[...]
    total[...] = loss_in[...]
    for halo, is_high in ((ze, 1 - pz), (zo, pz)):
        widez[...] = halo[REACH * rows :].reshape(widez.shape).astype(F32)
        for p in range(REACH):
            at = 2 * rows * p
            labz[p] = widez[at : at + rows] * 256.0 + widez[at + rows : at + 2 * rows]
        weight = (is_high * pos[2]).astype(F32)
        for o in OFFSETS:

            @pl.loop(0, o, unroll=True)
            def _(t):
                p = t + is_high * (planes - o)
                q = t + (1 - is_high) * (REACH - o)
                other = halo[pl.ds(q * rows, rows)].astype(F32)
                slopes, losses = pair_terms(
                    dots(emb[p].astype(F32), other),
                    lab[p].astype(F32) == labz[q],
                )
                grad[p] += slopes[:, None, :] * other
                total[:rows] += losses * weight


def outer_kernel(
    pos,
    emb,
    lab,
    grad,
    loss_in,
    fe,
    fo,
    ye,
    yo,
    ext,
    out,
    ge,
    go,
    packed,
    shifted,
    total,
    laby,
    wide,
    halos,
    acc,
):
    planes, rows = emb.shape[0], emb.shape[1]
    pz, py = pos[0], pos[1]
    channels, lanes = emb.shape[2], emb.shape[3]
    third = channels
    cells = (planes - 2) * (REACH - 1)
    total[...] = loss_in[...]
    for halo, side in ((fe, 1 - py), (fo, py)):
        wide[...] = halo[cells:].reshape(wide.shape).astype(F32)
        for z in range(planes):
            at = 2 * REACH * z
            laby[side, z] = wide[at : at + REACH] * 256.0 + wide[at + REACH : at + 2 * REACH]

    shifted[:, :2] = jnp.zeros((planes, 2) + shifted.shape[2:], BF)
    shifted[:, rows + 2 :] = jnp.zeros((planes, 2) + shifted.shape[2:], BF)
    for early, late, is_high in ((fe, ye, 1 - py), (fo, yo, py)):
        halos[is_high, 0] = late[:REACH]
        halos[is_high, planes - 1] = late[REACH : 2 * REACH]
        halos[is_high, 1 : planes - 1, (1 - is_high) * (REACH - 1)] = late[2 * REACH :]
        part = early[: (planes - 2) * (REACH - 1)]
        halos[is_high, 1 : planes - 1, pl.ds(is_high, REACH - 1)] = part.reshape(
            planes - 2, REACH - 1, *part.shape[1:]
        )
    live = pos[3].astype(F32)

    @pl.loop(0, planes, unroll=True)
    def _(z):
        center = emb[z].astype(F32)
        here = lab[z].astype(F32)
        sum_z = grad[z]
        low = halos[0, z].astype(F32)
        high = halos[1, z].astype(F32)
        lower, upper = [], []
        for o in OFFSETS:
            lower.append((center[:o], low[REACH - o :], here[:o], laby[0, z, REACH - o :]))
            upper.append((center[rows - o :], high[:o], here[rows - o :], laby[1, z, :o]))
        logits = [dots(a, b) for a, b, _, _ in lower + upper]
        mine = jnp.concatenate([c for _, _, c, _ in lower + upper], axis=0)
        theirs = jnp.concatenate([d for _, _, _, d in lower + upper], axis=0)
        slopes, losses = pair_terms(jnp.concatenate(logits, axis=0), mine == theirs)
        half = sum(OFFSETS)
        total[:1] += jnp.sum(losses[half:], axis=0, keepdims=True) * live
        at = 0
        for o, (_, other, _, _) in zip(OFFSETS, lower):
            sum_z = jnp.concatenate(
                [sum_z[:o] + slopes[at : at + o, None, :] * other, sum_z[o:]], axis=0
            )
            at += o
        for o, (_, other, _, _) in zip(OFFSETS, upper):
            sum_z = jnp.concatenate(
                [
                    sum_z[: rows - o],
                    sum_z[rows - o :] + slopes[at : at + o, None, :] * other,
                ],
                axis=0,
            )
            at += o
        value = sum_z.astype(BF)
        out[z] = value
        wide = value.astype(F32)
        shifted[z, 2 : rows + 2, :third] = lane_shift(wide, 1).astype(BF)
        shifted[z, 2 : rows + 2, third : 2 * third] = value
        shifted[z, 2 : rows + 2, 2 * third :] = lane_shift(wide, -1).astype(BF)

    ge[...] = out[(1 - pz) * (planes - 1)]
    go[...] = out[pz * (planes - 1)]

    acc[...] = jnp.zeros_like(acc)

    @pl.loop(0, planes, unroll=True)
    def _(z):
        products = acc[...]
        for y in range(0, rows + 2, 2):
            left = jnp.concatenate(
                [
                    jnp.concatenate([shifted[z, y + i + 2 - b] for b in range(3)], axis=0)
                    for i in range(2)
                ],
                axis=1,
            )
            right = jnp.concatenate(
                [
                    jnp.concatenate([ext[z + a, y + i] for a in range(3)], axis=0)
                    for i in range(2)
                ],
                axis=1,
            )
            products = products + lax.dot_general(
                left, right, (((1,), (1,)), ((), ())), preferred_element_type=F32
            )
        acc[...] = products

    height, width = acc.shape
    packed[...] = jnp.zeros_like(packed)
    packed[:height, :width] = acc[...]
    tile = jnp.sum(out[...].astype(F32), axis=(0, 1))
    column = jnp.sum(tile, axis=1, keepdims=True)
    row = lax.broadcasted_iota(jnp.int32, (channels, lanes), 0)
    lane = lax.broadcasted_iota(jnp.int32, (channels, lanes), 1)
    line = jnp.sum(jnp.where(row == lane, column, 0.0), axis=0, keepdims=True)
    first = lax.broadcasted_iota(jnp.int32, (1, lanes), 1)
    packed[height : height + 1, :] = jnp.where(first == channels, jnp.sum(total[...], keepdims=True), line)


def backward_kernel(pos, own, ye, yo, ze, zo, w, after, out, ext):
    planes, rows = own.shape[0], own.shape[1]
    ext[1 : planes + 1, 1 : rows + 1] = own[...]
    fill_rim(ext, ze, zo, ye, yo, pos[0], pos[1])

    @pl.loop(0, planes, unroll=True)
    def _(z):
        for y in range(0, rows, 2):
            for i, value in conv_rows(ext, w, z, (y, y + 1)):
                out[z, i] = value.astype(BF)


def spread_kernel(parts, out):
    out[...] = jnp.broadcast_to(jnp.sum(parts[...], axis=0), out.shape)


def final_kernel(voxels, pair_count, total, out, bias, loss):
    groups, channels, width = out.shape
    per = groups // 3
    height = per * channels
    for a in range(3):
        part = total[:height, a * width : (a + 1) * width] * (1.0 / voxels)
        out[a * per : (a + 1) * per] = part.reshape(per, channels, width)
    bias[...] = total[height : height + 1, :channels] * (1.0 / voxels)
    loss[...] = total[height : height + 1, channels : channels + 1] * (1.0 / pair_count)


def per_device(features, labels, weight, conv_bias):
    ch_in, planes, rows, lanes = features.shape
    emb_ch = weight.shape[0]
    gz, gy = lax.axis_size("gz"), lax.axis_size("gy")
    depth, height = planes * gz, rows * gy
    voxels = depth * height * lanes
    pair_count = sum(
        (extent - o) * (voxels // extent)
        for extent in (depth, height, lanes)
        for o in OFFSETS
        if o < extent
    )
    iz, iy = lax.axis_index("gz"), lax.axis_index("gy")
    pos = jnp.stack(
        [
            lax.rem(iz, 2),
            lax.rem(iy, 2),
            (iz < gz - 1).astype(jnp.int32),
            (iy < gy - 1).astype(jnp.int32),
        ]
    ).astype(jnp.int32)
    z_even, z_odd = even_pairs(gz), odd_pairs(gz)
    y_even, y_odd = even_pairs(gy), odd_pairs(gy)

    feat = jnp.transpose(features, (1, 2, 0, 3))
    taps = jnp.transpose(weight, (2, 3, 4, 0, 1))
    w_fwd = jnp.transpose(taps, (2, 3, 0, 1, 4)).reshape(3 * emb_ch, 9 * ch_in)
    w_bwd = jnp.transpose(taps[::-1, ::-1, ::-1], (2, 4, 0, 1, 3)).reshape(
        3 * ch_in, 9 * emb_ch
    )
    bias = jnp.broadcast_to(conv_bias[:, None], (emb_ch, lanes))

    sds = jax.ShapeDtypeStruct
    tile = (emb_ch, lanes)
    cells = (ch_in, lanes)
    z_blocks = -(-2 * REACH * rows // ch_in)
    y_blocks = -(-2 * REACH * planes // ch_in)

    z_message = sds((rows,) + cells, BF)
    me, mo = call(
        first_kernel,
        (z_message, z_message),
        (pos, feat),
        [SM, pl.BlockSpec(memory_space=pltpu.HBM)],
        scratch=[pltpu.SemaphoreType.DMA((2,))],
    )
    fze = lax.ppermute(me, "gz", z_even)
    fzo = lax.ppermute(mo, "gz", z_odd)
    emb_shape = sds((planes, rows) + tile, BF)
    ext_shape = sds((planes + 2, rows + 2) + cells, BF)
    y_early = sds(
        ((planes - 2) * (REACH - 1) + y_blocks * (ch_in // emb_ch),) + tile, BF
    )
    z_labels = sds((z_blocks * (ch_in // emb_ch),) + tile, BF)
    emb_part, me, mo, lze, lzo = call(
        second_kernel,
        (emb_shape, y_early, y_early, z_labels, z_labels),
        (pos, feat, labels, w_fwd, bias),
        [SM] + [VM] * 4,
        scratch=[
            pltpu.VMEM((y_blocks * ch_in, lanes), F32),
            pltpu.VMEM((z_blocks * ch_in, lanes), F32),
        ],
        micros=3.4,
    )
    aye = lax.ppermute(me, "gy", y_even)
    ayo = lax.ppermute(mo, "gy", y_odd)
    y_message = sds((planes + 2,) + cells, BF)
    me, mo = call(
        edge_rows, (y_message, y_message), (pos, feat, fze, fzo, me), [SM] + [VM] * 3 + [HELD]
    )
    fye = lax.ppermute(me, "gy", y_even)
    fyo = lax.ppermute(mo, "gy", y_odd)

    z_halo = sds((REACH * rows + z_labels.shape[0],) + tile, BF)
    y_late = sds((2 * REACH + planes - 2,) + tile, BF)
    emb, feat_ext, se, so, te, to = call(
        forward_kernel,
        (emb_shape, ext_shape, z_halo, z_halo, y_late, y_late),
        (pos, emb_part, feat, fze, fzo, fye, fyo, w_fwd, bias, lze, lzo),
        [SM] + [VM] * 10,
        micros=3.6,
    )
    eze = lax.ppermute(se, "gz", z_even)
    ezo = lax.ppermute(so, "gz", z_odd)
    eye = lax.ppermute(te, "gy", y_even)
    eyo = lax.ppermute(to, "gy", y_odd)

    lost_rows = -(-rows // 8) * 8
    grad_shape = sds((planes, rows) + tile, F32)
    loss_shape = sds((lost_rows, lanes), F32)
    grad_a, loss_a = call(
        inner_kernel,
        (grad_shape, loss_shape),
        (emb, labels, aye, ayo),
        [VM] * 2 + [HELD] * 2,
        micros=4.0,
    )
    grad_b, loss_b = call(
        outer_z_kernel,
        (grad_shape, loss_shape),
        (pos, emb, labels, grad_a, loss_a, eze, ezo),
        [SM] + [VM] * 6,
        scratch=[
            pltpu.VMEM((REACH, rows, lanes), F32),
            pltpu.VMEM((z_blocks * ch_in, lanes), F32),
        ],
        micros=1.5,
    )
    used = 9 * emb_ch + 1
    padded = -(-used // (8 * gz)) * 8 * gz
    share = padded // gz
    grad, ge, go, partial = call(
        outer_kernel,
        (
            sds((planes, rows) + tile, BF),
            sds((rows,) + tile, BF),
            sds((rows,) + tile, BF),
            sds((padded, lanes), F32),
        ),
        (pos, emb, labels, grad_b, loss_b, aye, ayo, eye, eyo, feat_ext),
        [SM] + [VM] * 9,
        scratch=[
            pltpu.VMEM((planes, rows + 4, 3 * emb_ch, lanes), BF),
            pltpu.VMEM((lost_rows, lanes), F32),
            pltpu.VMEM((2, planes, REACH, lanes), F32),
            pltpu.VMEM((y_blocks * ch_in, lanes), F32),
            pltpu.VMEM((2, planes, REACH) + tile, BF),
            pltpu.VMEM((9 * emb_ch, 3 * ch_in), F32),
        ],
        micros=3.7,
    )
    gze = lax.ppermute(ge, "gz", z_even)
    gzo = lax.ppermute(go, "gz", z_odd)

    y_edge = sds((planes + 2,) + tile, BF)
    me, mo = call(
        edge_rows, (y_edge, y_edge), (pos, grad, gze, gzo, ge), [SM] + [VM] * 3 + [HELD]
    )
    gye = lax.ppermute(me, "gy", y_even)
    gyo = lax.ppermute(mo, "gy", y_odd)

    parts = lax.all_to_all(partial.reshape(gz, share, lanes), "gz", 0, 0)
    mine = call(spread_kernel, sds((gy, share, lanes), F32), (parts,), [VM])
    feature_grad = call(
        backward_kernel,
        sds((planes, rows) + cells, BF),
        (pos, grad, gye, gyo, gze, gzo, w_bwd, mine),
        [SM] + [VM] * 6 + [HELD],
        scratch=[pltpu.VMEM((planes + 2, rows + 2) + tile, BF)],
        micros=4.9,
    )
    parts = lax.all_to_all(mine, "gy", 0, 0)
    mine = call(spread_kernel, sds((gz, share, lanes), F32), (parts,), [VM])
    total = lax.all_to_all(mine, "gz", 0, 0).reshape(padded, lanes)

    weight_grad, bias_grad, loss = call(
        functools.partial(final_kernel, voxels, pair_count),
        (sds((27, emb_ch, ch_in), F32), sds((1, emb_ch), F32), sds((1, 1), F32)),
        (total,),
        [VM],
    )
    weight_grad = jnp.transpose(
        weight_grad.reshape(3, 3, 3, emb_ch, ch_in), (3, 4, 0, 1, 2)
    )
    return (
        jnp.transpose(feature_grad, (2, 0, 1, 3)),
        weight_grad,
        bias_grad.reshape(emb_ch),
        loss.reshape(()),
    )


def solution(mesh):
    return jax.shard_map(
        per_device,
        mesh=mesh,
        in_specs=(P(None, "gz", "gy", None), P("gz", "gy", None), P(), P()),
        out_specs=(P(None, "gz", "gy", None), P(), P(), P()),
        check_vma=False,
    )
```

```python
import functools

import jax
import jax.numpy as jnp
from jax import lax
from jax.experimental import pallas as pl
from jax.experimental.pallas import tpu as pltpu
from jax.sharding import PartitionSpec as P

OFFSETS = (1, 3, 9)
REACH = 9
BF = jnp.bfloat16
F32 = jnp.float32
PEAK = 1.15e9
PARAMS = pltpu.CompilerParams(vmem_limit_bytes=48 * 1024 * 1024)
VM = pl.BlockSpec(memory_space=pltpu.VMEM)
HELD = pl.BlockSpec(memory_space=pl.ANY)
SM = pl.BlockSpec(memory_space=pltpu.SMEM)


def call(body, outs, args, specs, scratch=(), micros=1.0):
    return pl.pallas_call(
        body,
        out_shape=outs,
        in_specs=specs,
        out_specs=jax.tree.map(lambda _: VM, outs),
        scratch_shapes=list(scratch),
        compiler_params=PARAMS,
        name=getattr(body, "__name__", "final_kernel"),
        cost_estimate=pl.CostEstimate(
            flops=int(micros * PEAK), bytes_accessed=1, transcendentals=0
        ),
    )(*args)


def even_pairs(count):
    return [(i, i ^ 1) for i in range(count - count % 2)]


def odd_pairs(count):
    pairs = [(i, i + 1) for i in range(1, count - 1, 2)]
    return pairs + [(j, i) for i, j in pairs]


def lane_shift(value, step):
    lanes = value.shape[-1]
    moved = pltpu.roll(value, (-step) % lanes, value.ndim - 1)
    lane = lax.broadcasted_iota(jnp.int32, value.shape, value.ndim - 1)
    keep = (lane < lanes - step) if step > 0 else (lane >= -step)
    return jnp.where(keep, moved, 0)


def pair_terms(logits, same):
    target = same.astype(F32)
    small = jnp.exp(-jnp.abs(logits))
    inverse = 1.0 / (1.0 + small)
    sigmoid = jnp.where(logits >= 0, inverse, small * inverse)
    slopes = (sigmoid - target) * 0.25
    losses = jnp.maximum(logits, 0.0) + jnp.log1p(small) - target * logits
    return slopes, losses


def dots(left, right):
    count = left.shape[0]
    parts = []
    for i in range(count):
        part = left[i] * right[i]
        parts.append(part[:8] + part[8:])
    parts += [None] * (-count % 8)
    sub = lax.broadcasted_iota(jnp.int32, parts[0].shape, 0)
    for step in (1, 2, 4):
        own = jnp.bitwise_and(sub, step) == 0
        merged = []
        for first, second in zip(parts[::2], parts[1::2]):
            if first is None:
                merged.append(None)
            elif second is None:
                merged.append(first + pltpu.roll(first, 8 - step, 0))
            else:
                merged.append(
                    jnp.where(own, first, second)
                    + pltpu.roll(jnp.where(own, second, first), 8 - step, 0)
                )
        parts = merged
    return jnp.concatenate(parts, axis=0)[:count] * 0.25


def fill_rim(ext, ze, zo, ye, yo, pz, py):
    planes, rows = ext.shape[0] - 2, ext.shape[1] - 2
    ext[(1 - pz) * (planes + 1), 1 : rows + 1] = ze[...]
    ext[pz * (planes + 1), 1 : rows + 1] = zo[...]
    ext[:, (1 - py) * (rows + 1)] = ye[...]
    ext[:, py * (rows + 1)] = yo[...]


def conv_rows(ext, w_ref, z, rows):
    stack = [
        jnp.concatenate([ext[z + a, y + b] for y in rows], axis=1)
        for a in range(3)
        for b in range(3)
    ]
    sums = jnp.dot(w_ref[...], jnp.concatenate(stack, axis=0), preferred_element_type=F32)
    third = sums.shape[0] // 3
    lanes = sums.shape[1] // len(rows)
    for i, y in enumerate(rows):
        part = sums[:, i * lanes : (i + 1) * lanes]
        yield (
            y,
            lane_shift(part[:third], -1)
            + part[third : 2 * third]
            + lane_shift(part[2 * third :], 1),
        )


def pack_labels(wide, blocks):
    at = 0
    for block in blocks:
        count = block.shape[0]
        wide[at : at + count] = lax.shift_right_logical(block, 8).astype(F32)
        wide[at + count : at + 2 * count] = jnp.bitwise_and(block, 255).astype(F32)
        at += 2 * count
    if at < wide.shape[0]:
        wide[at:] = jnp.zeros((wide.shape[0] - at, wide.shape[1]), F32)


def first_kernel(pos, feat, even, odd, sems):
    pz, planes = pos[0], feat.shape[0]
    copies = [
        pltpu.make_async_copy(feat.at[(1 - pz) * (planes - 1)], even, sems.at[0]),
        pltpu.make_async_copy(feat.at[pz * (planes - 1)], odd, sems.at[1]),
    ]
    for copy in copies:
        copy.start()
    for copy in copies:
        copy.wait()


def second_kernel(pos, feat, lab, w, bias, emb, even, odd, lze, lzo, wide, widez):
    planes, rows = feat.shape[0], feat.shape[1]
    pz, py = pos[0], pos[1]
    for out, high in ((lze, 1 - pz), (lzo, pz)):
        base = high * (planes - REACH)
        pack_labels(widez, [lab[base + p] for p in range(REACH)])
        out[...] = widez[...].astype(BF).reshape(out.shape)
    cells = (planes - 2) * (REACH - 1)
    for out, high in ((even, 1 - py), (odd, py)):
        pack_labels(
            wide,
            [
                jnp.where(high == 1, lab[z, rows - REACH :], lab[z, :REACH])
                for z in range(planes)
            ],
        )
        out[cells:] = wide[...].astype(BF).reshape(out.shape[0] - cells, *out.shape[1:])

    @pl.loop(0, planes - 2, unroll=True)
    def _(z):
        for y in range(0, rows - 2, 2):
            for i, value in conv_rows(feat, w, z, (y, y + 1)):
                emb[z + 1, i + 1] = (value + bias[...]).astype(BF)

    for out, high in ((even, 1 - py), (odd, py)):
        part = emb[1 : planes - 1, pl.ds(1 + high * (rows - 1 - REACH), REACH - 1)]
        out[:cells] = part.reshape(cells, *part.shape[2:])


def edge_rows(pos, own, ze, zo, after, even, odd):
    planes, rows = own.shape[0], own.shape[1]
    pz, py = pos[0], pos[1]
    for out, high in ((even, 1 - py), (odd, py)):
        row = high * (rows - 1)
        out[1 : planes + 1] = own[:, row]
        out[(1 - pz) * (planes + 1)] = ze[row]
        out[pz * (planes + 1)] = zo[row]


def forward_kernel(
    pos, part, feat, ze, zo, yo, ye, w, bias, lze, lzo, emb, ext, se, so, te, to
):
    planes, rows = emb.shape[0], emb.shape[1]
    pz, py = pos[0], pos[1]
    ext[1 : planes + 1, 1 : rows + 1] = feat[...]
    fill_rim(ext, ze, zo, ye, yo, pz, py)
    emb[1 : planes - 1, 1 : rows - 1] = part[1 : planes - 1, 1 : rows - 1]

    @pl.loop(0, planes, unroll=True)
    def _(z):
        for i, value in conv_rows(ext, w, z, (0, rows - 1)):
            emb[z, i] = (value + bias[...]).astype(BF)

    @pl.loop(0, 2, unroll=True)
    def _(side):
        z = side * (planes - 1)
        for y in range(1, rows - 1, 2):
            for i, value in conv_rows(ext, w, z, (y, y + 1)):
                emb[z, i] = (value + bias[...]).astype(BF)

    for out, labels, high in ((se, lze, 1 - pz), (so, lzo, pz)):
        halo = emb[pl.ds(high * (planes - REACH), REACH)]
        out[: REACH * rows] = halo.reshape(REACH * rows, *halo.shape[2:])
        out[REACH * rows :] = labels[...]
    for out, high in ((te, 1 - py), (to, py)):
        part = pl.ds(high * (rows - REACH), REACH)
        out[:REACH] = emb[0, part]
        out[REACH : 2 * REACH] = emb[planes - 1, part]
        out[2 * REACH :] = emb[1 : planes - 1, high * (rows - 1)]


def inner_kernel(emb, lab, ao, ae, grad, loss):
    planes, rows = emb.shape[0], emb.shape[1]
    lanes = emb.shape[3]
    lane = lax.broadcasted_iota(jnp.int32, (rows, lanes), 1)
    loss[...] = jnp.zeros_like(loss)

    @pl.loop(0, planes, unroll=2)
    def _(z):
        center = emb[z].astype(F32)
        here = lab[z]
        total = jnp.zeros(center.shape, F32)
        lost = jnp.zeros((rows, lanes), F32)
        for o in OFFSETS:
            if o < lanes:
                after = pltpu.roll(center, lanes - o, 2)
                before = pltpu.roll(center, o, 2)
                live = lane < lanes - o
                slopes, losses = pair_terms(
                    dots(center, after), here == pltpu.roll(here, lanes - o, 1)
                )
                slopes = jnp.where(live, slopes, 0.0)
                lost = lost + jnp.where(live, losses, 0.0)
                total = total + slopes[:, None, :] * after
                total = total + pltpu.roll(slopes, o, 1)[:, None, :] * before
        grad[z] = total
        for o in OFFSETS:
            if o < rows:
                low, high = center[: rows - o], center[o:]
                slopes, losses = pair_terms(dots(low, high), here[: rows - o] == here[o:])
                grad[z, : rows - o] += slopes[:, None, :] * high
                grad[z, o:] += slopes[:, None, :] * low
                loss[: rows - o] += losses
        loss[:rows] += lost

    for o in OFFSETS:

        @pl.loop(0, planes - o, unroll=True)
        def _(z):
            low, high = emb[z].astype(F32), emb[z + o].astype(F32)
            slopes, losses = pair_terms(dots(low, high), lab[z] == lab[z + o])
            grad[z] += slopes[:, None, :] * high
            grad[z + o] += slopes[:, None, :] * low
            loss[:rows] += losses


def outer_z_kernel(pos, emb, lab, grad_in, loss_in, ze, zo, grad, total, labz, widez):
    planes, rows = emb.shape[0], emb.shape[1]
    pz = pos[0]
    grad[...] = grad_in[...]
    total[...] = loss_in[...]
    for halo, is_high in ((ze, 1 - pz), (zo, pz)):
        widez[...] = halo[REACH * rows :].reshape(widez.shape).astype(F32)
        for p in range(REACH):
            at = 2 * rows * p
            labz[p] = widez[at : at + rows] * 256.0 + widez[at + rows : at + 2 * rows]
        weight = (is_high * pos[2]).astype(F32)
        for o in OFFSETS:

            @pl.loop(0, o, unroll=True)
            def _(t):
                p = t + is_high * (planes - o)
                q = t + (1 - is_high) * (REACH - o)
                other = halo[pl.ds(q * rows, rows)].astype(F32)
                slopes, losses = pair_terms(
                    dots(emb[p].astype(F32), other),
                    lab[p].astype(F32) == labz[q],
                )
                grad[p] += slopes[:, None, :] * other
                total[:rows] += losses * weight


def outer_kernel(
    pos,
    emb,
    lab,
    grad,
    loss_in,
    fo,
    fe,
    yo,
    ye,
    ext,
    out,
    ge,
    go,
    packed,
    shifted,
    total,
    laby,
    wide,
    halos,
    acc,
):
    planes, rows = emb.shape[0], emb.shape[1]
    pz, py = pos[0], pos[1]
    channels, lanes = emb.shape[2], emb.shape[3]
    third = channels
    cells = (planes - 2) * (REACH - 1)
    total[...] = loss_in[...]
    for halo, side in ((fe, 1 - py), (fo, py)):
        wide[...] = halo[cells:].reshape(wide.shape).astype(F32)
        for z in range(planes):
            at = 2 * REACH * z
            laby[side, z] = wide[at : at + REACH] * 256.0 + wide[at + REACH : at + 2 * REACH]

    shifted[:, :2] = jnp.zeros((planes, 2) + shifted.shape[2:], BF)
    shifted[:, rows + 2 :] = jnp.zeros((planes, 2) + shifted.shape[2:], BF)
    for early, late, is_high in ((fe, ye, 1 - py), (fo, yo, py)):
        halos[is_high, 0] = late[:REACH]
        halos[is_high, planes - 1] = late[REACH : 2 * REACH]
        halos[is_high, 1 : planes - 1, (1 - is_high) * (REACH - 1)] = late[2 * REACH :]
        part = early[: (planes - 2) * (REACH - 1)]
        halos[is_high, 1 : planes - 1, pl.ds(is_high, REACH - 1)] = part.reshape(
            planes - 2, REACH - 1, *part.shape[1:]
        )
    live = pos[3].astype(F32)

    @pl.loop(0, planes, unroll=True)
    def _(z):
        center = emb[z].astype(F32)
        here = lab[z].astype(F32)
        sum_z = grad[z]
        low = halos[0, z].astype(F32)
        high = halos[1, z].astype(F32)
        lower, upper = [], []
        for o in OFFSETS:
            lower.append((center[:o], low[REACH - o :], here[:o], laby[0, z, REACH - o :]))
            upper.append((center[rows - o :], high[:o], here[rows - o :], laby[1, z, :o]))
        logits = [dots(a, b) for a, b, _, _ in lower + upper]
        mine = jnp.concatenate([c for _, _, c, _ in lower + upper], axis=0)
        theirs = jnp.concatenate([d for _, _, _, d in lower + upper], axis=0)
        slopes, losses = pair_terms(jnp.concatenate(logits, axis=0), mine == theirs)
        half = sum(OFFSETS)
        total[:1] += jnp.sum(losses[half:], axis=0, keepdims=True) * live
        at = 0
        for o, (_, other, _, _) in zip(OFFSETS, lower):
            sum_z = jnp.concatenate(
                [sum_z[:o] + slopes[at : at + o, None, :] * other, sum_z[o:]], axis=0
            )
            at += o
        for o, (_, other, _, _) in zip(OFFSETS, upper):
            sum_z = jnp.concatenate(
                [
                    sum_z[: rows - o],
                    sum_z[rows - o :] + slopes[at : at + o, None, :] * other,
                ],
                axis=0,
            )
            at += o
        value = sum_z.astype(BF)
        out[z] = value
        wide = value.astype(F32)
        shifted[z, 2 : rows + 2, :third] = lane_shift(wide, 1).astype(BF)
        shifted[z, 2 : rows + 2, third : 2 * third] = value
        shifted[z, 2 : rows + 2, 2 * third :] = lane_shift(wide, -1).astype(BF)

    ge[...] = out[(1 - pz) * (planes - 1)]
    go[...] = out[pz * (planes - 1)]

    acc[...] = jnp.zeros_like(acc)

    @pl.loop(0, planes, unroll=True)
    def _(z):
        products = acc[...]
        for y in range(0, rows + 2, 2):
            left = jnp.concatenate(
                [
                    jnp.concatenate([shifted[z, y + i + 2 - b] for b in range(3)], axis=0)
                    for i in range(2)
                ],
                axis=1,
            )
            right = jnp.concatenate(
                [
                    jnp.concatenate([ext[z + a, y + i] for a in range(3)], axis=0)
                    for i in range(2)
                ],
                axis=1,
            )
            products = products + lax.dot_general(
                left, right, (((1,), (1,)), ((), ())), preferred_element_type=F32
            )
        acc[...] = products

    height, width = acc.shape
    packed[...] = jnp.zeros_like(packed)
    packed[:height, :width] = acc[...]
    tile = jnp.sum(out[...].astype(F32), axis=(0, 1))
    column = jnp.sum(tile, axis=1, keepdims=True)
    row = lax.broadcasted_iota(jnp.int32, (channels, lanes), 0)
    lane = lax.broadcasted_iota(jnp.int32, (channels, lanes), 1)
    line = jnp.sum(jnp.where(row == lane, column, 0.0), axis=0, keepdims=True)
    first = lax.broadcasted_iota(jnp.int32, (1, lanes), 1)
    packed[height : height + 1, :] = jnp.where(first == channels, jnp.sum(total[...], keepdims=True), line)


def backward_kernel(pos, own, yo, ye, ze, zo, w, after, out, ext):
    planes, rows = own.shape[0], own.shape[1]
    ext[1 : planes + 1, 1 : rows + 1] = own[...]
    fill_rim(ext, ze, zo, ye, yo, pos[0], pos[1])

    @pl.loop(0, planes, unroll=True)
    def _(z):
        for y in range(0, rows, 2):
            for i, value in conv_rows(ext, w, z, (y, y + 1)):
                out[z, i] = value.astype(BF)


def spread_kernel(parts, out):
    out[...] = jnp.broadcast_to(jnp.sum(parts[...], axis=0), out.shape)


def final_kernel(voxels, pair_count, total, out, bias, loss):
    groups, channels, width = out.shape
    per = groups // 3
    height = per * channels
    for a in range(3):
        part = total[:height, a * width : (a + 1) * width] * (1.0 / voxels)
        out[a * per : (a + 1) * per] = part.reshape(per, channels, width)
    bias[...] = total[height : height + 1, :channels] * (1.0 / voxels)
    loss[...] = total[height : height + 1, channels : channels + 1] * (1.0 / pair_count)


def per_device(features, labels, weight, conv_bias):
    ch_in, planes, rows, lanes = features.shape
    emb_ch = weight.shape[0]
    gz, gy = lax.axis_size("gz"), lax.axis_size("gy")
    depth, height = planes * gz, rows * gy
    voxels = depth * height * lanes
    pair_count = sum(
        (extent - o) * (voxels // extent)
        for extent in (depth, height, lanes)
        for o in OFFSETS
        if o < extent
    )
    iz, iy = lax.axis_index("gz"), lax.axis_index("gy")
    pos = jnp.stack(
        [
            lax.rem(iz, 2),
            lax.rem(iy, 2),
            (iz < gz - 1).astype(jnp.int32),
            (iy < gy - 1).astype(jnp.int32),
        ]
    ).astype(jnp.int32)
    z_even, z_odd = even_pairs(gz), odd_pairs(gz)
    y_even, y_odd = even_pairs(gy), odd_pairs(gy)

    feat = jnp.transpose(features, (1, 2, 0, 3))
    taps = jnp.transpose(weight, (2, 3, 4, 0, 1))
    w_fwd = jnp.transpose(taps, (2, 3, 0, 1, 4)).reshape(3 * emb_ch, 9 * ch_in)
    w_bwd = jnp.transpose(taps[::-1, ::-1, ::-1], (2, 4, 0, 1, 3)).reshape(
        3 * ch_in, 9 * emb_ch
    )
    bias = jnp.broadcast_to(conv_bias[:, None], (emb_ch, lanes))

    sds = jax.ShapeDtypeStruct
    tile = (emb_ch, lanes)
    cells = (ch_in, lanes)
    z_blocks = -(-2 * REACH * rows // ch_in)
    y_blocks = -(-2 * REACH * planes // ch_in)

    z_message = sds((rows,) + cells, BF)
    me, mo = call(
        first_kernel,
        (z_message, z_message),
        (pos, feat),
        [SM, pl.BlockSpec(memory_space=pltpu.HBM)],
        scratch=[pltpu.SemaphoreType.DMA((2,))],
    )
    fze = lax.ppermute(me, "gz", z_even)
    fzo = lax.ppermute(mo, "gz", z_odd)
    emb_shape = sds((planes, rows) + tile, BF)
    ext_shape = sds((planes + 2, rows + 2) + cells, BF)
    y_early = sds(
        ((planes - 2) * (REACH - 1) + y_blocks * (ch_in // emb_ch),) + tile, BF
    )
    z_labels = sds((z_blocks * (ch_in // emb_ch),) + tile, BF)
    emb_part, me, mo, lze, lzo = call(
        second_kernel,
        (emb_shape, y_early, y_early, z_labels, z_labels),
        (pos, feat, labels, w_fwd, bias),
        [SM] + [VM] * 4,
        scratch=[
            pltpu.VMEM((y_blocks * ch_in, lanes), F32),
            pltpu.VMEM((z_blocks * ch_in, lanes), F32),
        ],
        micros=3.4,
    )
    aye = lax.ppermute(me, "gy", y_even)
    ayo = lax.ppermute(mo, "gy", y_odd)
    y_message = sds((planes + 2,) + cells, BF)
    me, mo = call(
        edge_rows, (y_message, y_message), (pos, feat, fze, fzo, me), [SM] + [VM] * 3 + [HELD]
    )
    fye = lax.ppermute(me, "gy", y_even)
    fyo = lax.ppermute(mo, "gy", y_odd)

    z_halo = sds((REACH * rows + z_labels.shape[0],) + tile, BF)
    y_late = sds((2 * REACH + planes - 2,) + tile, BF)
    emb, feat_ext, se, so, te, to = call(
        forward_kernel,
        (emb_shape, ext_shape, z_halo, z_halo, y_late, y_late),
        (pos, emb_part, feat, fze, fzo, fyo, fye, w_fwd, bias, lze, lzo),
        [SM] + [VM] * 10,
        micros=3.6,
    )
    eze = lax.ppermute(se, "gz", z_even)
    ezo = lax.ppermute(so, "gz", z_odd)
    eye = lax.ppermute(te, "gy", y_even)
    eyo = lax.ppermute(to, "gy", y_odd)

    lost_rows = -(-rows // 8) * 8
    grad_shape = sds((planes, rows) + tile, F32)
    loss_shape = sds((lost_rows, lanes), F32)
    grad_a, loss_a = call(
        inner_kernel,
        (grad_shape, loss_shape),
        (emb, labels, ayo, aye),
        [VM] * 2 + [HELD] * 2,
        micros=4.0,
    )
    grad_b, loss_b = call(
        outer_z_kernel,
        (grad_shape, loss_shape),
        (pos, emb, labels, grad_a, loss_a, eze, ezo),
        [SM] + [VM] * 6,
        scratch=[
            pltpu.VMEM((REACH, rows, lanes), F32),
            pltpu.VMEM((z_blocks * ch_in, lanes), F32),
        ],
        micros=1.5,
    )
    used = 9 * emb_ch + 1
    padded = -(-used // (8 * gz)) * 8 * gz
    share = padded // gz
    grad, ge, go, partial = call(
        outer_kernel,
        (
            sds((planes, rows) + tile, BF),
            sds((rows,) + tile, BF),
            sds((rows,) + tile, BF),
            sds((padded, lanes), F32),
        ),
        (pos, emb, labels, grad_b, loss_b, ayo, aye, eyo, eye, feat_ext),
        [SM] + [VM] * 9,
        scratch=[
            pltpu.VMEM((planes, rows + 4, 3 * emb_ch, lanes), BF),
            pltpu.VMEM((lost_rows, lanes), F32),
            pltpu.VMEM((2, planes, REACH, lanes), F32),
            pltpu.VMEM((y_blocks * ch_in, lanes), F32),
            pltpu.VMEM((2, planes, REACH) + tile, BF),
            pltpu.VMEM((9 * emb_ch, 3 * ch_in), F32),
        ],
        micros=3.7,
    )
    gze = lax.ppermute(ge, "gz", z_even)
    gzo = lax.ppermute(go, "gz", z_odd)

    y_edge = sds((planes + 2,) + tile, BF)
    me, mo = call(
        edge_rows, (y_edge, y_edge), (pos, grad, gze, gzo, ge), [SM] + [VM] * 3 + [HELD]
    )
    gye = lax.ppermute(me, "gy", y_even)
    gyo = lax.ppermute(mo, "gy", y_odd)

    parts = lax.all_to_all(partial.reshape(gz, share, lanes), "gz", 0, 0)
    mine = call(spread_kernel, sds((gy, share, lanes), F32), (parts,), [VM])
    feature_grad = call(
        backward_kernel,
        sds((planes, rows) + cells, BF),
        (pos, grad, gyo, gye, gze, gzo, w_bwd, mine),
        [SM] + [VM] * 6 + [HELD],
        scratch=[pltpu.VMEM((planes + 2, rows + 2) + tile, BF)],
        micros=4.9,
    )
    parts = lax.all_to_all(mine, "gy", 0, 0)
    mine = call(spread_kernel, sds((gz, share, lanes), F32), (parts,), [VM])
    total = lax.all_to_all(mine, "gz", 0, 0).reshape(padded, lanes)

    weight_grad, bias_grad, loss = call(
        functools.partial(final_kernel, voxels, pair_count),
        (sds((27, emb_ch, ch_in), F32), sds((1, emb_ch), F32), sds((1, 1), F32)),
        (total,),
        [VM],
    )
    weight_grad = jnp.transpose(
        weight_grad.reshape(3, 3, 3, emb_ch, ch_in), (3, 4, 0, 1, 2)
    )
    return (
        jnp.transpose(feature_grad, (2, 0, 1, 3)),
        weight_grad,
        bias_grad.reshape(emb_ch),
        loss.reshape(()),
    )


def solution(mesh):
    return jax.shard_map(
        per_device,
        mesh=mesh,
        in_specs=(P(None, "gz", "gy", None), P("gz", "gy", None), P(), P()),
        out_specs=(P(None, "gz", "gy", None), P(), P(), P()),
        check_vma=False,
    )
```
